128 devices in a mesh: row: 16 (over x_lo, z, core), col: 8 (over x_hi, y).
Axes of the slice: x: 4 (x_hi: 2, x_lo: 2; x = x_hi * 2 + x_lo), y: 4, z: 4, core: 2. Of those that a mesh axis runs over, the one named last changes fastest.
Arguments:
- atom_single: bfloat16 [16384, 128], P(('row', 'col')), may hold values from -60 to 60
- atom_to_token: int32 [16384], replicated, may hold values from 0 to 2047, as said below
- token_mask: int32 [2048], P('col'), may hold values 0 or 1
- pair: bfloat16 [2048, 2048, 128], P('row', 'col'), may hold values from -16 to 16
- w_atom_qkv: bfloat16 [128, 384], replicated, may hold values from -0.5 to 0.5
- w_atom_out: bfloat16 [128, 128], replicated, may hold values from -0.5 to 0.5
- w_aggregate: bfloat16 [128, 768], replicated, may hold values from -0.5 to 0.5
- pair_gain: float32 [128], replicated, may hold values from 0.1 to 1.9
- w_pair_in: bfloat16 [128, 512], replicated, may hold values from -0.5 to 0.5
- w_pair_out: bfloat16 [256, 128], replicated, may hold values from -0.375 to 0.375
- bias_gain: float32 [128], replicated, may hold values from 0.15 to 200
- w_bias: bfloat16 [128, 16], replicated, may hold values from -2 to 2
- token_gain: float32 [768], replicated, may hold values from 0.1 to 1.9
- w_token_qkv: bfloat16 [768, 2304], replicated, may hold values from -0.21875 to 0.21875
- w_token_out: bfloat16 [768, 768], replicated, may hold values from -0.21875 to 0.21875
Outputs:
- atom_out: bfloat16 [16384, 128], P(('row', 'col'))
- token_out: bfloat16 [2048, 768], P(('row', 'col'))
- pair_out: bfloat16 [2048, 2048, 128], P('row', 'col')
The draws below stay inside these ranges and needn't reach their ends.
Inputs may be any that keep to these rules, and one draw needn't show every extreme that they name: `atom_to_token`: never falling; every token 0 to 2047 has 1 to 24 atoms, some token exactly 24.
All inputs are finite; a program needn't handle non-finite values. No bound on the sum of `token_mask` on one device may be relied on, other than what follows from the above.
Results may differ from the reference program's by a relative error of at most 0.018.
Values may be sent and summed in bfloat16 or wider, within the bound.
A program may use at most 128 MiB of HBM per device.

```python
import jax
import jax.numpy as jnp
from jax import lax

AH = 4
AHD = 32
TH = 16
TD = 48
PC = 128
ATOM_QUERIES = 32
ATOM_KEYS = 128
MAXA = 24
ATOM_WIDTH = 128
TW = 768
PH = 256
TOKENS = 2048
TOTAL_ATOMS = 16384
QB = 128


def draw_atom_to_token(key, part):
    key = jax.random.fold_in(key, 15)
    heavy = (TOTAL_ATOMS - TOKENS) * 15 // (16 * (MAXA - 1))
    light = TOKENS - heavy
    extra = TOTAL_ATOMS - TOKENS - heavy * (MAXA - 1)
    slots = jax.random.permutation(key, light * (MAXA - 1))[:extra]
    owner = slots // (MAXA - 1)
    light_counts = 1 + jnp.zeros((light,), jnp.int32).at[owner].add(1)
    counts = jnp.concatenate([jnp.full((heavy,), MAXA, jnp.int32), light_counts])
    ends = jnp.cumsum(counts).astype(jnp.int32)
    return jnp.searchsorted(ends, jnp.arange(TOTAL_ATOMS, dtype=jnp.int32), side='right').astype(jnp.int32)


def draw_atom_single(key, part):
    key = jax.random.fold_in(key, 11)
    key_base = jax.random.fold_in(key, 0)
    return jnp.clip(jax.random.normal(key_base, (TOTAL_ATOMS, ATOM_WIDTH), jnp.float32), -6.0, 6.0).astype(jnp.bfloat16)


def draw_pair(key, part):
    key = jax.random.fold_in(key, 12)
    key_base = jax.random.fold_in(key, 0)
    return jnp.clip(jax.random.normal(key_base, (TOKENS, TOKENS, PC), jnp.float32), -6.0, 6.0).astype(jnp.bfloat16)


def draw_bias_gain(key, part):
    key = jax.random.fold_in(key, 13)
    return 1.0 + 0.18 * jnp.clip(jax.random.normal(key, (PC,), jnp.float32), -4.5, 4.5)


def draw_w_bias(key, part):
    key = jax.random.fold_in(key, 14)
    key_main = jax.random.fold_in(key, 0)
    return (jnp.clip(jax.random.normal(key_main, (PC, TH), jnp.float32), -6.0, 6.0) * PC ** (-0.5)).astype(jnp.bfloat16)


def touch_ends(values, key, smallest, largest):
    index_at = [jax.random.randint(jax.random.fold_in(key, axis), (), 0, length) for axis, length in enumerate(values.shape)]
    longest = values.shape.index(max(values.shape))
    next_to = index_at[:longest] + [(index_at[longest] + 1) % values.shape[longest]] + index_at[longest + 1:]
    return values.at[tuple(index_at)].set(smallest).at[tuple(next_to)].set(largest)


def gaussian(key, dims, width, bound, kind=jnp.bfloat16):
    return jnp.clip(width * jax.random.normal(key, dims, jnp.float32), -bound, bound).astype(kind)


def setup_inputs(seed: int = 0) -> dict:
    splits = jax.random.split(jax.random.key(seed), 16)
    return {
        "atom_single": draw_atom_single(jax.random.fold_in(splits[15], 71), 0),
        "atom_to_token": draw_atom_to_token(jax.random.fold_in(splits[15], 71), 0),
        "token_mask": touch_ends((jax.random.randint(splits[2], (TOKENS,), 0, 8) < 7).astype(jnp.int32), jax.random.fold_in(splits[2], 1), 0, 1),
        "pair": draw_pair(jax.random.fold_in(splits[15], 71), 0),
        "w_atom_qkv": gaussian(splits[4], (ATOM_WIDTH, 3 * ATOM_WIDTH), ATOM_WIDTH ** -0.5, 0.5),
        "w_atom_out": gaussian(splits[5], (ATOM_WIDTH, ATOM_WIDTH), ATOM_WIDTH ** -0.5, 0.5),
        "w_aggregate": gaussian(splits[6], (ATOM_WIDTH, TW), ATOM_WIDTH ** -0.5, 0.5),
        "pair_gain": jnp.clip(1.0 + 0.18 * jax.random.normal(splits[7], (PC,), jnp.float32), 0.1, 1.9),
        "w_pair_in": gaussian(splits[8], (PC, 2 * PH), PC ** -0.5, 0.5),
        "w_pair_out": gaussian(splits[9], (PH, PC), PH ** -0.5, 0.375),
        "bias_gain": draw_bias_gain(jax.random.fold_in(splits[15], 71), 0),
        "w_bias": draw_w_bias(jax.random.fold_in(splits[15], 71), 0),
        "token_gain": jnp.clip(1.0 + 0.18 * jax.random.normal(splits[12], (TW,), jnp.float32), 0.1, 1.9),
        "w_token_qkv": gaussian(splits[13], (TW, 3 * TW), TW ** -0.5, 0.21875),
        "w_token_out": gaussian(splits[14], (TW, TW), TW ** -0.5, 0.21875),
    }


def layer_norm(x, gain):
    mean = lax.optimization_barrier(jnp.mean(x, axis=-1, keepdims=True))
    var = lax.optimization_barrier(jnp.mean((x - mean) ** 2, axis=-1, keepdims=True))
    return (x - mean) / jnp.sqrt(var + 1e-05) * gain

def reference(atom_single, atom_to_token, token_mask, pair, w_atom_qkv, w_atom_out, w_aggregate, pair_gain, w_pair_in, w_pair_out, bias_gain, w_bias, token_gain, w_token_qkv, w_token_out):
    atom_qkv = jnp.dot(atom_single, w_atom_qkv, preferred_element_type=jnp.float32).astype(jnp.bfloat16)
    nblock = TOTAL_ATOMS // ATOM_QUERIES
    query = atom_qkv[:, :ATOM_WIDTH].reshape(nblock, ATOM_QUERIES, AH, AHD)
    padded = jnp.pad(atom_qkv[:, ATOM_WIDTH:], ((48, 48), (0, 0)))
    index = ATOM_QUERIES * jnp.arange(nblock, dtype=jnp.int32)[:, None] + jnp.arange(ATOM_KEYS, dtype=jnp.int32)[None, :]
    window = padded[index]
    keys = window[:, :, :ATOM_WIDTH].reshape(nblock, ATOM_KEYS, AH, AHD)
    values = window[:, :, ATOM_WIDTH:].reshape(nblock, ATOM_KEYS, AH, AHD)
    place = index - 48
    outside = jnp.where((place >= 0) & (place < TOTAL_ATOMS), 0.0, -1000000000.0).astype(jnp.float32)
    scores = jnp.einsum('bqhd,bkhd->bhqk', query.astype(jnp.float32), keys.astype(jnp.float32)) / jnp.sqrt(jnp.float32(AHD))
    scores = scores + outside[:, None, None, :]
    expo = jnp.exp(scores - lax.optimization_barrier(jnp.max(scores, axis=-1, keepdims=True)))
    total = lax.optimization_barrier(jnp.sum(expo, axis=-1))
    numer = jnp.einsum('bhqk,bkhd->bqhd', expo.astype(jnp.bfloat16).astype(jnp.float32), values.astype(jnp.float32))
    atom_mix = (numer / jnp.transpose(total, (0, 2, 1))[..., None]).astype(jnp.bfloat16).reshape(TOTAL_ATOMS, ATOM_WIDTH)
    atom_out = (atom_single.astype(jnp.float32) + jnp.dot(atom_mix, w_atom_out, preferred_element_type=jnp.float32)).astype(jnp.bfloat16)
    atom_proj = jax.nn.relu(jnp.dot(atom_out, w_aggregate, preferred_element_type=jnp.float32)).astype(jnp.bfloat16)
    sums = jax.ops.segment_sum(atom_proj.astype(jnp.float32), atom_to_token, TOKENS)
    counts = jax.ops.segment_sum(jnp.ones((TOTAL_ATOMS,), jnp.float32), atom_to_token, TOKENS)
    token_in = (sums / counts[:, None]).astype(jnp.bfloat16)

    def pair_rows(block):
        normed = layer_norm(block.astype(jnp.float32), pair_gain).astype(jnp.bfloat16)
        both = jnp.dot(normed, w_pair_in, preferred_element_type=jnp.float32)
        hidden = (jax.nn.silu(both[..., :PH]) * both[..., PH:]).astype(jnp.bfloat16)
        new_pair = (block.astype(jnp.float32) + jnp.dot(hidden, w_pair_out, preferred_element_type=jnp.float32)).astype(jnp.bfloat16)
        normed_two = layer_norm(new_pair.astype(jnp.float32), bias_gain).astype(jnp.bfloat16)
        bias = jnp.dot(normed_two, w_bias, preferred_element_type=jnp.float32)
        return (new_pair, bias)
    pair_out, pair_bias = lax.map(pair_rows, pair.reshape(TOKENS // 16, 16, TOKENS, PC))
    pair_out = pair_out.reshape(TOKENS, TOKENS, PC)
    pair_bias = pair_bias.reshape(TOKENS, TOKENS, TH)
    token_norm = layer_norm(token_in.astype(jnp.float32), token_gain).astype(jnp.bfloat16)
    token_qkv = jnp.dot(token_norm, w_token_qkv, preferred_element_type=jnp.float32).astype(jnp.bfloat16)
    tkeys = token_qkv[:, TW:2 * TW].reshape(TOKENS, TH, TD).astype(jnp.float32)
    tvalues = token_qkv[:, 2 * TW:].reshape(TOKENS, TH, TD).astype(jnp.float32)
    masking = (token_mask.astype(jnp.float32) - 1.0) * 1000000000.0

    def query_rows(inputs):
        tquery, bias = inputs
        tscores = jnp.einsum('qhd,khd->hqk', tquery.reshape(QB, TH, TD).astype(jnp.float32), tkeys) / jnp.sqrt(jnp.float32(TD))
        tscores = tscores + jnp.transpose(bias, (2, 0, 1)) + masking[None, None, :]
        texpo = jnp.exp(tscores - lax.optimization_barrier(jnp.max(tscores, axis=-1, keepdims=True)))
        ttotal = lax.optimization_barrier(jnp.sum(texpo, axis=-1))
        tnumer = jnp.einsum('hqk,khd->qhd', texpo.astype(jnp.bfloat16).astype(jnp.float32), tvalues)
        return (tnumer / jnp.transpose(ttotal)[..., None]).astype(jnp.bfloat16).reshape(QB, TW)
    token_mix = lax.map(query_rows, (token_qkv[:, :TW].reshape(TOKENS // QB, QB, TW), pair_bias.reshape(TOKENS // QB, QB, TOKENS, TH)))
    token_mix = token_mix.reshape(TOKENS, TW)
    token_out = (token_in.astype(jnp.float32) + jnp.dot(token_mix, w_token_out, preferred_element_type=jnp.float32)).astype(jnp.bfloat16)
    return (atom_out, token_out, pair_out)
```

```python
import functools

import jax
import jax.numpy as jnp
from jax import lax
from jax.experimental import pallas as pl
from jax.experimental.pallas import tpu as pltpu
from jax.sharding import PartitionSpec as P

F32, BF16 = jnp.float32, jnp.bfloat16
MESH = pl.DeviceIdType.MESH
NT = (((1,), (1,)), ((), ()))
ROWS, COLS = 16, 8
WINDOW, KEYS, HALO = 32, 128, 48
ATOM_HEADS, TOKEN_HEADS, HEAD = 4, 16, 48
OWN = 16
VMEM_LIMIT = 48 << 20


def dot(a, b):
    return jnp.dot(a, b, preferred_element_type=F32)


def dot_nt(a, b):
    return lax.dot_general(a, b, NT, preferred_element_type=F32)


def remote(src, dst, send, recv, row, col):
    return pltpu.make_async_remote_copy(
        src_ref=src, dst_ref=dst, send_sem=send, recv_sem=recv,
        device_id=(row, col), device_id_type=MESH,
    )


def greet(sem, row, col):
    pl.semaphore_signal(sem, inc=1, device_id=(row, col), device_id_type=MESH)


def atom_attention(x, me, atoms_total, w_qkv, w_out):
    n = 128
    qkv = dot(x, w_qkv).astype(BF16)
    q = qkv[HALO:HALO + n, :128]
    k, v = qkv[:, 128:256], qkv[:, 256:]
    pad = jnp.zeros((256 - k.shape[0], 128), BF16)
    k = jnp.concatenate([k, pad], axis=0)
    v = jnp.concatenate([v, pad], axis=0)
    lane = lax.broadcasted_iota(jnp.int32, (n, 128), 1)
    parts = []
    for h in range(ATOM_HEADS):
        keep = (lane >= 32 * h) & (lane < 32 * h + 32)
        parts.append(jnp.where(keep, q.astype(F32), 0.0).astype(BF16))
    s = dot_nt(jnp.concatenate(parts, axis=0), k) * (32.0 ** -0.5)
    atom = lax.broadcasted_iota(jnp.int32, (n, 256), 0)
    key = lax.broadcasted_iota(jnp.int32, (n, 256), 1)
    first = (atom // WINDOW) * WINDOW
    place = key - HALO + me * n
    shift = jnp.where((place >= 0) & (place < atoms_total), 0.0, -1e9)
    inside = (key >= first) & (key < first + KEYS)
    out = jnp.zeros((n, 128), F32)
    for h in range(ATOM_HEADS):
        sh = jnp.where(inside, s[h * n:(h + 1) * n] + shift, -1e30)
        e = jnp.exp(sh - jnp.max(sh, axis=-1, keepdims=True))
        total = jnp.sum(e, axis=-1, keepdims=True)
        o = dot(e.astype(BF16), v) / total
        keep = (lane >= 32 * h) & (lane < 32 * h + 32)
        out = jnp.where(keep, o, out)
    own = x[HALO:HALO + n].astype(F32)
    return (own + dot(out.astype(BF16), w_out)).astype(BF16)


def tokens_kernel(
    atom_ref, ids_ref, w_aqkv, w_aout, w_agg, gain, w_qkv,
    atom_out_ref, token_ref, q_ref, k_ref, v_ref,
    x_buf, gathered, sums, parts, norm, tq, tk,
    halo_s, halo_r, gat_s, gat_r, sum_s, sum_r, tq_s, tq_r, tk_s, tk_r,
):
    row, col = lax.axis_index("row"), lax.axis_index("col")
    me = row * COLS + col
    left, right = (me + 127) % 128, (me + 1) % 128
    key_col = row // 2
    mine = (key_col == col).astype(jnp.int32)

    barrier = pltpu.get_barrier_semaphore()
    greet(barrier, left // COLS, left % COLS)
    greet(barrier, right // COLS, right % COLS)
    for d in range(1, ROWS):
        greet(barrier, (row + d) % ROWS, col)
    for d in range(1, COLS):
        greet(barrier, row, (col + d) % COLS)
    for s in range(16):
        r2, c2 = 2 * col + s // COLS, s % COLS

        @pl.when((r2 != row) | (c2 != col))
        def _():
            greet(barrier, r2, c2)

    x_buf[HALO:HALO + 128] = atom_ref[...]
    pl.semaphore_wait(barrier, 2 + 15 + 7 + 16 - mine)

    to_right = remote(atom_ref.at[pl.ds(80, 48)], x_buf.at[pl.ds(0, 48)],
                      halo_s.at[0], halo_r.at[0], right // COLS, right % COLS)
    to_left = remote(atom_ref.at[pl.ds(0, 48)], x_buf.at[pl.ds(176, 48)],
                     halo_s.at[1], halo_r.at[1], left // COLS, left % COLS)
    to_right.start()
    to_left.start()

    own_tokens = me * OWN + lax.broadcasted_iota(jnp.int32, (OWN, 128), 0)

    def count_step(i, acc):
        ids = ids_ref[pl.ds(i * 8, 8), :]
        for t in range(8):
            acc = acc + (own_tokens == ids[t:t + 1]).astype(F32)
        return acc

    counts = lax.fori_loop(0, 16, count_step, jnp.zeros((OWN, 128), F32))
    count = jnp.sum(counts, axis=-1, keepdims=True)
    to_right.wait()
    to_left.wait()

    atom_out = atom_attention(x_buf[...], me, 128 * 128, w_aqkv[...], w_aout[...])
    atom_out_ref[...] = atom_out
    gathered[pl.ds(row, 1)] = atom_out[None]

    def gather(d):
        return remote(gathered.at[row], gathered.at[row], gat_s.at[d], gat_r.at[row],
                      (row + d) % ROWS, col)

    def gather_in(d):
        j = (row + d) % ROWS
        return remote(gathered.at[j], gathered.at[j], gat_s.at[d], gat_r.at[j], row, col)

    for d in range(1, ROWS):
        gather(d).start()
    for d in range(1, ROWS):
        gather_in(d).wait_recv()

    token = row * 128 + lax.broadcasted_iota(jnp.int32, (128, 128), 0)
    total = jnp.zeros((128, 768), F32)
    for j in range(0, ROWS, 2):
        a = jnp.concatenate([gathered[j], gathered[j + 1]], axis=0)
        proj = jnp.maximum(dot(a, w_agg[...]), 0.0).astype(BF16)
        hot = [
            (token == ids_ref[pl.ds(COLS * (j + t) + col, 1), :]).astype(F32).astype(BF16)
            for t in range(2)
        ]
        total = total + dot(jnp.concatenate(hot, axis=1), proj)
    sums[...] = total.reshape(COLS, OWN, 768)

    def send_sum(d):
        c2 = (col + d) % COLS
        return remote(sums.at[c2], parts.at[col], sum_s.at[d], sum_r.at[col], row, c2)

    def recv_sum(d):
        c2 = (col + d) % COLS
        return remote(sums.at[c2], parts.at[c2], sum_s.at[d], sum_r.at[c2], row, col)

    for d in range(1, COLS):
        send_sum(d).start()
    parts[pl.ds(col, 1)] = sums[pl.ds(col, 1)]
    for d in range(1, COLS):
        recv_sum(d).wait_recv()
    acc = parts[0]
    for s in range(1, COLS):
        acc = acc + parts[s]
    token_in = (acc / count).astype(BF16)
    token_ref[...] = token_in
    t = token_in.astype(F32)
    tc = t - jnp.mean(t, axis=-1, keepdims=True)
    var = jnp.mean(tc * tc, axis=-1, keepdims=True)
    norm[...] = (tc * lax.rsqrt(var + 1e-5) * gain[...]).astype(BF16)
    tq[pl.ds(col, 1)] = norm[...][None]
    slot = COLS * (row % 2) + col

    def send_q(d):
        return remote(norm, tq.at[col], tq_s.at[d], tq_r.at[col], row, (col + d) % COLS)

    def recv_q(d):
        c2 = (col + d) % COLS
        return remote(norm, tq.at[c2], tq_s.at[d], tq_r.at[c2], row, col)

    def send_k(d):
        return remote(norm, tk.at[slot], tk_s.at[d], tk_r.at[slot], (row + d) % ROWS, key_col)

    def recv_k(s):
        return remote(norm, tk.at[s], tk_s.at[s], tk_r.at[s], row, col)

    for d in range(1, ROWS):
        send_k(d).start()

    @pl.when(mine == 0)
    def _():
        send_k(0).start()

    @pl.when(mine == 1)
    def _():
        tk[pl.ds(slot, 1)] = norm[...][None]

    for d in range(1, COLS):
        send_q(d).start()
    for d in range(1, COLS):
        recv_q(d).wait_recv()
    tqv = tq[...].reshape(128, 768)
    q_ref[...] = dot(tqv, w_qkv[:, :768]).astype(BF16)
    for s in range(16):
        @pl.when((2 * col + s // COLS != row) | (s % COLS != col))
        def _():
            recv_k(s).wait_recv()

    tkv = tk[...].reshape(256, 768)
    k_ref[...] = dot(tkv, w_qkv[:, 768:1536]).astype(BF16)
    v_ref[...] = dot(tkv, w_qkv[:, 1536:]).astype(BF16)

    for d in range(1, ROWS):
        gather(d).wait_send()
        send_k(d).wait_send()
    for d in range(1, COLS):
        send_sum(d).wait_send()
        send_q(d).wait_send()

    @pl.when(mine == 0)
    def _():
        send_k(0).wait_send()


def norm_rows(x_bf, gain, ones):
    x = x_bf.astype(F32)
    xc = x - dot(x_bf, ones)
    var = jnp.mean(xc * xc, axis=-1, keepdims=True)
    return x, (xc * lax.rsqrt(var + 1e-5) * gain).astype(BF16)


def pair_kernel(x_ref, w_in, w_out, w_bias, g_pair, g_bias, ones, out_ref, bias_ref):
    n, keys, chan = x_ref.shape
    x, normed = norm_rows(x_ref[...].reshape(n * keys, chan), g_pair[...], ones[...])
    both = dot(normed, w_in[...])
    half, up = both[:, :256], both[:, 256:]
    hidden = ((half + half * jnp.tanh(half)) * up).astype(BF16)
    new = (x + dot(hidden, w_out[...])).astype(BF16)
    out_ref[...] = new.reshape(n, keys, chan)
    _, normed = norm_rows(new, g_bias[...], ones[...])
    for t in range(n):
        bias_ref[16 * t:16 * t + 16, :] = dot_nt(w_bias[...], normed[t * keys:(t + 1) * keys])


def pair_step(pair, w_in, w_out, w_bias, g_pair, g_bias):
    nq, keys, chan = pair.shape
    block = 16
    hidden = w_out.shape[0]
    w_in = jnp.concatenate([w_in[:, :hidden] * jnp.asarray(0.5, BF16), w_in[:, hidden:]], axis=1)
    ones = jnp.full((chan, chan), 1.0 / chan, BF16)

    def whole(a):
        return pl.BlockSpec(a.shape, lambda i: (0,) * a.ndim)

    weights = (w_in, w_out, w_bias.T, g_pair.reshape(1, chan), g_bias.reshape(1, chan), ones)
    return pl.pallas_call(
        pair_kernel,
        grid=(nq // block,),
        in_specs=[pl.BlockSpec((block, keys, chan), lambda i: (i, 0, 0))] + [whole(a) for a in weights],
        out_specs=[
            pl.BlockSpec((block, keys, chan), lambda i: (i, 0, 0)),
            pl.BlockSpec((block * 16, keys), lambda i: (i, 0)),
        ],
        out_shape=[
            jax.ShapeDtypeStruct(pair.shape, BF16),
            jax.ShapeDtypeStruct((nq * 16, keys), F32),
        ],
        compiler_params=pltpu.CompilerParams(vmem_limit_bytes=VMEM_LIMIT),
        name="pair",
    )(pair, *weights)


def attend_kernel(
    q_ref, k_ref, v_ref, bias_ref, mask_ref, w_out, token_ref,
    out_ref,
    num_out, st_out, num_in, st_in, num_s, num_r, st_s, st_r,
):
    row, col = lax.axis_index("row"), lax.axis_index("col")
    barrier = pltpu.get_barrier_semaphore()
    for d in range(1, COLS):
        greet(barrier, row, (col + d) % COLS)

    head = lax.broadcasted_iota(jnp.int32, (16, 768), 0)
    lane = lax.broadcasted_iota(jnp.int32, (16, 768), 1)
    heads = jnp.where((lane >= head * HEAD) & (lane < head * HEAD + HEAD), 1.0, 0.0)
    eye = jnp.where(
        lax.broadcasted_iota(jnp.int32, (16, 128), 0) == lax.broadcasted_iota(jnp.int32, (16, 128), 1),
        1.0, 0.0,
    )
    masking = (mask_ref[...].astype(F32) - 1.0) * 1e9

    def chunk(c2):
        qs = q_ref[pl.ds(c2 * OWN, OWN), :].astype(F32)
        big = (qs[:, None, :] * heads[None]).reshape(256, 768).astype(BF16)
        s = dot_nt(big, k_ref[...]) * (HEAD ** -0.5)
        s = s + bias_ref[pl.ds(c2 * 256, 256), :] + masking
        top = jnp.max(s, axis=-1, keepdims=True)
        e = jnp.exp(s - top)
        total = jnp.sum(e, axis=-1, keepdims=True)
        o = dot(e.astype(BF16), v_ref[...])
        num = jnp.sum(o.reshape(OWN, 16, 768) * heads[None], axis=1)
        tops = jnp.sum(jnp.broadcast_to(top, (256, 128)).reshape(OWN, 16, 128) * eye[None], axis=1)
        totals = jnp.sum(jnp.broadcast_to(total, (256, 128)).reshape(OWN, 16, 128) * eye[None], axis=1)
        return num.astype(BF16), jnp.concatenate([tops, totals], axis=0)

    def send(d):
        c2 = (col + d) % COLS
        return (
            remote(num_out.at[c2], num_in.at[col], num_s.at[d], num_r.at[col], row, c2),
            remote(st_out.at[c2], st_in.at[col], st_s.at[d], st_r.at[col], row, c2),
        )

    def receive(d):
        c2 = (col + d) % COLS
        return (
            remote(num_out.at[c2], num_in.at[c2], num_s.at[d], num_r.at[c2], row, col),
            remote(st_out.at[c2], st_in.at[c2], st_s.at[d], st_r.at[c2], row, col),
        )

    for d in range(1, COLS):
        c2 = (col + d) % COLS
        num, st = chunk(c2)
        num_out[pl.ds(c2, 1)] = num[None]
        st_out[pl.ds(c2, 1)] = st[None]
        if d == 1:
            pl.semaphore_wait(barrier, COLS - 1)
        for copy in send(d):
            copy.start()
    num, st = chunk(col)
    num_in[pl.ds(col, 1)] = num[None]
    st_in[pl.ds(col, 1)] = st[None]
    for d in range(1, COLS):
        for copy in receive(d):
            copy.wait_recv()
    st = st_in[...]
    tops, totals = st[:, :OWN], st[:, OWN:]
    best = jnp.max(tops, axis=0, keepdims=True)
    w = jnp.exp(tops - best)
    den = jnp.sum(w * totals, axis=0)
    small = jnp.concatenate([w.reshape(COLS * OWN, 128), den], axis=0)
    wide = jnp.concatenate([heads, jnp.zeros((112, 768), F32)], axis=0)
    spread = jnp.dot(small, wide, preferred_element_type=F32, precision=lax.Precision.HIGHEST)
    num = jnp.zeros((OWN, 768), F32)
    for s in range(COLS):
        num = num + num_in[s].astype(F32) * spread[s * OWN:(s + 1) * OWN]
    mix = (num / spread[COLS * OWN:]).astype(BF16)
    out_ref[...] = (token_ref[...].astype(F32) + dot(mix, w_out[...])).astype(BF16)
    for d in range(1, COLS):
        for copy in send(d):
            copy.wait_send()


def body(
    atom_single, atom_to_token, token_mask, pair, w_atom_qkv, w_atom_out, w_aggregate,
    pair_gain, w_pair_in, w_pair_out, bias_gain, w_bias, token_gain, w_token_qkv, w_token_out,
):
    vmem = pl.BlockSpec(memory_space=pltpu.VMEM)
    dma = pltpu.SemaphoreType.DMA
    atom_out, token_in, q, k, v = pl.pallas_call(
        tokens_kernel,
        in_specs=[vmem] * 7,
        out_specs=[vmem] * 5,
        out_shape=[
            jax.ShapeDtypeStruct((128, 128), BF16),
            jax.ShapeDtypeStruct((OWN, 768), BF16),
            jax.ShapeDtypeStruct((128, 768), BF16),
            jax.ShapeDtypeStruct((256, 768), BF16),
            jax.ShapeDtypeStruct((256, 768), BF16),
        ],
        scratch_shapes=[
            pltpu.VMEM((224, 128), BF16),
            pltpu.VMEM((ROWS, 128, 128), BF16),
            pltpu.VMEM((COLS, OWN, 768), F32),
            pltpu.VMEM((COLS, OWN, 768), F32),
            pltpu.VMEM((OWN, 768), BF16),
            pltpu.VMEM((COLS, OWN, 768), BF16),
            pltpu.VMEM((16, OWN, 768), BF16),
            dma((2,)), dma((2,)), dma((ROWS,)), dma((ROWS,)), dma((COLS,)), dma((COLS,)),
            dma((COLS,)), dma((COLS,)), dma((16,)), dma((16,)),
        ],
        compiler_params=pltpu.CompilerParams(
            collective_id=0, has_side_effects=True, vmem_limit_bytes=VMEM_LIMIT
        ),
        name="tokens",
    )(
        atom_single, atom_to_token.reshape(128, 128), w_atom_qkv, w_atom_out, w_aggregate,
        token_gain.reshape(1, 768), w_token_qkv,
    )
    pair_out, bias = pair_step(pair, w_pair_in, w_pair_out, w_bias, pair_gain, bias_gain)
    token_out = pl.pallas_call(
        attend_kernel,
        in_specs=[vmem] * 7,
        out_specs=vmem,
        out_shape=jax.ShapeDtypeStruct((OWN, 768), BF16),
        scratch_shapes=[
            pltpu.VMEM((COLS, OWN, 768), BF16),
            pltpu.VMEM((COLS, 2 * OWN, 128), F32),
            pltpu.VMEM((COLS, OWN, 768), BF16),
            pltpu.VMEM((COLS, 2 * OWN, 128), F32),
            dma((COLS,)), dma((COLS,)), dma((COLS,)), dma((COLS,)),
        ],
        compiler_params=pltpu.CompilerParams(
            collective_id=1, has_side_effects=True, vmem_limit_bytes=VMEM_LIMIT
        ),
        name="attend",
    )(q, k, v, bias, token_mask.reshape(1, 256), w_token_out, token_in)
    return (atom_out, token_out, pair_out)


def solution(mesh):
    atoms = P(("row", "col"), None)
    pairs = P("row", "col", None)
    return jax.shard_map(
        body,
        mesh=mesh,
        in_specs=(atoms, P(), P("col"), pairs) + (P(),) * 11,
        out_specs=(atoms, atoms, pairs),
        check_vma=False,
    )
```

```python
import functools

import jax
import jax.numpy as jnp
from jax import lax
from jax.experimental import pallas as pl
from jax.experimental.pallas import tpu as pltpu
from jax.sharding import PartitionSpec as P

F32, BF16 = jnp.float32, jnp.bfloat16
MESH = pl.DeviceIdType.MESH
NT = (((1,), (1,)), ((), ()))
ROWS, COLS = 16, 8
WINDOW, KEYS, HALO = 32, 128, 48
ATOM_HEADS, TOKEN_HEADS, HEAD = 4, 16, 48
OWN = 16
VMEM_LIMIT = 56 << 20
SUM_TYPE = BF16
CHUNK = 16
EARLY = 7
STAGES = (0, 1, 3, 4, 5)


def dot(a, b):
    return jnp.dot(a, b, preferred_element_type=F32)


def dot_nt(a, b):
    return lax.dot_general(a, b, NT, preferred_element_type=F32)


def remote(src, dst, send, recv, row, col):
    return pltpu.make_async_remote_copy(
        src_ref=src, dst_ref=dst, send_sem=send, recv_sem=recv,
        device_id=(row, col), device_id_type=MESH,
    )


def greet(sem, row, col):
    pl.semaphore_signal(sem, inc=1, device_id=(row, col), device_id_type=MESH)


def atom_attention(x, me, atoms_total, w_qkv, w_out):
    n = 128
    qkv = dot(x, w_qkv).astype(BF16)
    q = qkv[HALO:HALO + n, :128]
    k, v = qkv[:, 128:256], qkv[:, 256:]
    pad = jnp.zeros((256 - k.shape[0], 128), BF16)
    k = jnp.concatenate([k, pad], axis=0)
    v = jnp.concatenate([v, pad], axis=0)
    lane = lax.broadcasted_iota(jnp.int32, (n, 128), 1)
    parts = []
    for h in range(ATOM_HEADS):
        keep = (lane >= 32 * h) & (lane < 32 * h + 32)
        parts.append(jnp.where(keep, q.astype(F32), 0.0).astype(BF16))
    s = dot_nt(jnp.concatenate(parts, axis=0), k) * (32.0 ** -0.5)
    atom = lax.broadcasted_iota(jnp.int32, (n, 256), 0)
    key = lax.broadcasted_iota(jnp.int32, (n, 256), 1)
    first = (atom // WINDOW) * WINDOW
    place = key - HALO + me * n
    shift = jnp.where((place >= 0) & (place < atoms_total), 0.0, -1e9)
    inside = (key >= first) & (key < first + KEYS)
    out = jnp.zeros((n, 128), F32)
    for h in range(ATOM_HEADS):
        sh = jnp.where(inside, s[h * n:(h + 1) * n] + shift, -1e30)
        e = jnp.exp(sh - jnp.max(sh, axis=-1, keepdims=True))
        total = jnp.sum(e, axis=-1, keepdims=True)
        o = dot(e.astype(BF16), v) / total
        keep = (lane >= 32 * h) & (lane < 32 * h + 32)
        out = jnp.where(keep, o, out)
    own = x[HALO:HALO + n].astype(F32)
    return (own + dot(out.astype(BF16), w_out)).astype(BF16)


def norm_rows(x_bf, gain, ones):
    x = x_bf.astype(F32)
    xc = x - dot(x_bf, ones)
    var = jnp.mean(xc * xc, axis=-1, keepdims=True)
    return x, (xc * lax.rsqrt(var + 1e-5) * gain).astype(BF16)


def pair_weights(w_in, half_in, ones):
    half_in[:, :256] = w_in[:, :256] * jnp.asarray(0.5, BF16)
    half_in[:, 256:] = w_in[:, 256:]
    ones[...] = jnp.full(ones.shape, 1.0 / 128.0, BF16)


def pair_chunk(x, w_in, w_out, bias_t, g_pair, g_bias, ones, put_bias):
    n, keys, chan = x.shape
    x, normed = norm_rows(x.reshape(n * keys, chan), g_pair[...], ones[...])
    both = dot(normed, w_in[...])
    half, up = both[:, :256], both[:, 256:]
    hidden = ((half + half * jnp.tanh(half)) * up).astype(BF16)
    new = (x + dot(hidden, w_out[...])).astype(BF16)
    _, normed = norm_rows(new, g_bias[...], ones[...])
    for t in range(n):
        put_bias(t, dot_nt(bias_t[...], normed[t * keys:(t + 1) * keys]))
    return new.reshape(n, keys, chan)


def token_norm(t, gain):
    gain = jnp.concatenate([gain[i:i + 1] for i in range(6)], axis=1)
    t = t.astype(F32)
    tc = t - jnp.mean(t, axis=-1, keepdims=True)
    var = jnp.mean(tc * tc, axis=-1, keepdims=True)
    return (tc * lax.rsqrt(var + 1e-5) * gain).astype(BF16)


def tokens_kernel(
    atom_hbm, ids_hbm, w_aqkv_hbm, w_aout_hbm, w_agg_hbm, gain_hbm, w_qkv_hbm,
    pair_hbm, w_in_hbm, w_out_hbm, bias_t_hbm, g_pair_hbm, g_bias_hbm,
    atom_out_ref, token_ref, q_ref, k_ref, v_ref, pair_out_hbm, bias_ref,
    atom, ids, w_aqkv, w_aout, w_agg, gain, w_qkv, w_in, w_out, bias_t, g_pair, g_bias,
    half_in, ones, pair_in, pair_new,
    x_buf, gathered, sums, parts, counts, key_token, own_token, key_norm, own_norm, tq, tk,
    load, pair_r, pair_w,
    halo_s, halo_r, gat_s, gat_r, sum_s, sum_r, move_s, move_r, tq_s, tq_r, tk_s, tk_r,
):
    row, col = lax.axis_index("row"), lax.axis_index("col")
    me = row * COLS + col
    left, right = (me + 127) % 128, (me + 1) % 128
    to_row, to_col = 2 * col + row // COLS, row % COLS
    from_row, from_col = COLS * (row % 2) + col, row // 2
    stays = ((to_row == row) & (to_col == col)).astype(jnp.int32)

    barrier = pltpu.get_barrier_semaphore()
    greet(barrier, left // COLS, left % COLS)
    greet(barrier, right // COLS, right % COLS)
    for d in range(1, ROWS):
        greet(barrier, (row + d) % ROWS, col)
    for d in range(1, COLS):
        greet(barrier, row, (col + d) % COLS)

    @pl.when(stays == 0)
    def _():
        greet(barrier, from_row, from_col)

    pairs = [
        (w_in_hbm, w_in), (w_out_hbm, w_out), (bias_t_hbm, bias_t), (g_pair_hbm, g_pair),
        (g_bias_hbm, g_bias), (atom_hbm, atom), (ids_hbm, ids), (w_aqkv_hbm, w_aqkv),
        (w_aout_hbm, w_aout), (w_agg_hbm, w_agg), (gain_hbm, gain), (w_qkv_hbm, w_qkv),
    ]
    loads = [pltpu.make_async_copy(a, b, load.at[i]) for i, (a, b) in enumerate(pairs)]
    chunks = pair_in.shape[0]

    def read(i):
        return pltpu.make_async_copy(
            pair_hbm.at[pl.ds(i * CHUNK, CHUNK)], pair_in.at[i], pair_r.at[i])

    def write(i):
        return pltpu.make_async_copy(
            pair_new.at[i], pair_out_hbm.at[pl.ds(i * CHUNK, CHUNK)], pair_w.at[i])

    for copy in loads[:5]:
        copy.start()
    read(0).start()
    for copy in loads[5:]:
        copy.start()
    for i in range(1, chunks):
        read(i).start()
    for copy in loads[:5]:
        copy.wait()
    pair_weights(w_in, half_in, ones)
    for copy in loads[5:]:
        copy.wait()
    x_buf[HALO:HALO + 128] = atom[...]

    to_right = remote(atom.at[pl.ds(80, 48)], x_buf.at[pl.ds(0, 48)],
                      halo_s.at[0], halo_r.at[0], right // COLS, right % COLS)
    to_left = remote(atom.at[pl.ds(0, 48)], x_buf.at[pl.ds(176, 48)],
                     halo_s.at[1], halo_r.at[1], left // COLS, left % COLS)

    def gather(d):
        return remote(gathered.at[row], gathered.at[row], gat_s.at[d], gat_r.at[row],
                      (row + d) % ROWS, col)

    def gather_in(d):
        j = (row + d) % ROWS
        return remote(gathered.at[j], gathered.at[j], gat_s.at[d], gat_r.at[j], row, col)

    def send_sum(d):
        c2 = (col + d) % COLS
        return remote(sums.at[c2], parts.at[col], sum_s.at[d], sum_r.at[col], row, c2)

    def recv_sum(d):
        c2 = (col + d) % COLS
        return remote(sums.at[c2], parts.at[c2], sum_s.at[d], sum_r.at[c2], row, col)

    move = remote(key_token, own_token, move_s.at[0], move_r.at[0], to_row, to_col)

    def send_q(d):
        return remote(own_norm, tq.at[col], tq_s.at[d], tq_r.at[col], row, (col + d) % COLS)

    def recv_q(d):
        c2 = (col + d) % COLS
        return remote(own_norm, tq.at[c2], tq_s.at[d], tq_r.at[c2], row, col)

    def send_k(d):
        return remote(key_norm, tk.at[row], tk_s.at[d], tk_r.at[row], (row + d) % ROWS, col)

    def recv_k(d):
        r2 = (row + d) % ROWS
        return remote(key_norm, tk.at[r2], tk_s.at[d], tk_r.at[r2], row, col)

    def start_halo():
        pl.semaphore_wait(barrier, 2 + 15 + 7 + 1 - stays)
        to_right.start()
        to_left.start()
        own_tokens = col * 256 + row * OWN + lax.broadcasted_iota(jnp.int32, (OWN, 128), 0)
        acc = jnp.zeros((OWN, 128), F32)
        for t in range(128):
            acc = acc + (own_tokens == ids[t:t + 1, :]).astype(F32)
        counts[...] = jnp.broadcast_to(jnp.sum(acc, axis=-1, keepdims=True), (OWN, 128))

    def start_gather():
        to_right.wait()
        to_left.wait()
        atom_out = atom_attention(x_buf[...], me, 128 * 128, w_aqkv[...], w_aout[...])
        atom_out_ref[...] = atom_out
        gathered[pl.ds(row, 1)] = atom_out[None]
        for d in range(1, ROWS):
            gather(d).start()

    def start_sums():
        for d in range(1, ROWS):
            gather_in(d).wait_recv()
        place = lax.broadcasted_iota(jnp.int32, (128, 128), 0)
        token = (place // OWN) * 256 + row * OWN + place % OWN
        total = jnp.zeros((128, 768), F32)
        for j in range(0, ROWS, 2):
            a = jnp.concatenate([gathered[j], gathered[j + 1]], axis=0)
            proj = jnp.maximum(dot(a, w_agg[...]), 0.0).astype(BF16)
            hot = [
                (token == ids[pl.ds(COLS * (j + t) + col, 1), :]).astype(F32).astype(BF16)
                for t in range(2)
            ]
            total = total + dot(jnp.concatenate(hot, axis=1), proj)
        sums[...] = total.astype(sums.dtype).reshape(COLS, OWN, 768)
        for d in range(1, COLS):
            send_sum(d).start()
        parts[pl.ds(col, 1)] = sums[pl.ds(col, 1)]

    def start_keys():
        for d in range(1, COLS):
            recv_sum(d).wait_recv()
        acc = parts[0].astype(F32)
        for s in range(1, COLS):
            acc = acc + parts[s].astype(F32)
        token_in = (acc / counts[:, :1]).astype(BF16)
        key_token[...] = token_in

        @pl.when(stays == 0)
        def _():
            move.start()

        @pl.when(stays == 1)
        def _():
            own_token[...] = token_in

        key_norm[...] = token_norm(token_in, gain[...])
        tk[pl.ds(row, 1)] = key_norm[...][None]
        for d in range(1, ROWS):
            send_k(d).start()

    def start_queries():
        @pl.when(stays == 0)
        def _():
            move.wait()

        token_ref[...] = own_token[...]
        own_norm[...] = token_norm(own_token[...], gain[...])
        tq[pl.ds(col, 1)] = own_norm[...][None]
        for d in range(1, COLS):
            send_q(d).start()

    def step(i, carry):
        read(i).wait()

        def put_bias(t, b):
            bias_ref[pl.ds(pl.multiple_of(i * CHUNK * 16 + 16 * t, 16), 16), :] = b

        pair_new[i] = pair_chunk(pair_in[i], half_in, w_out, bias_t, g_pair, g_bias, ones, put_bias)
        write(i).start()
        for at, stage in zip(STAGES, (start_halo, start_gather, start_sums, start_keys, start_queries)):
            pl.when(i == at)(stage)
        return carry

    lax.fori_loop(0, chunks, step, 0)

    for d in range(1, COLS):
        recv_q(d).wait_recv()
    tqv = tq[...].reshape(128, 768)
    q_ref[...] = dot(tqv, w_qkv[:, :768]).astype(BF16)
    for d in range(1, ROWS):
        recv_k(d).wait_recv()
    tkv = tk[...].reshape(256, 768)
    k_ref[...] = dot(tkv, w_qkv[:, 768:1536]).astype(BF16)
    v_ref[...] = dot(tkv, w_qkv[:, 1536:]).astype(BF16)

    for d in range(1, ROWS):
        gather(d).wait_send()
        send_k(d).wait_send()
    for d in range(1, COLS):
        send_sum(d).wait_send()
        send_q(d).wait_send()
    for i in range(chunks):
        write(i).wait()


def rest_kernel(
    pair_hbm, done_hbm, w_in, w_out, bias_t, g_pair, g_bias,
    out_hbm, bias_ref,
    half_in, ones, pair_in, pair_new, held, pair_r, pair_w, done_r, done_w,
):
    count, first = pair_in.shape[0], done_hbm.shape[0]

    def read(i):
        return pltpu.make_async_copy(
            pair_hbm.at[pl.ds(first + i * CHUNK, CHUNK)], pair_in.at[i], pair_r.at[i])

    def write(i):
        return pltpu.make_async_copy(
            pair_new.at[i], out_hbm.at[pl.ds(first + i * CHUNK, CHUNK)], pair_w.at[i])

    def fetch(i):
        return pltpu.make_async_copy(
            done_hbm.at[pl.ds(i * CHUNK, CHUNK)], held.at[i], done_r.at[i])

    def hand_on(i):
        return pltpu.make_async_copy(
            held.at[i], out_hbm.at[pl.ds(i * CHUNK, CHUNK)], done_w.at[i])

    for i in range(count):
        read(i).start()
    for i in range(first // CHUNK):
        fetch(i).start()
    pair_weights(w_in, half_in, ones)

    def step(i, carry):
        read(i).wait()

        def put_bias(t, b):
            bias_ref[pl.ds(pl.multiple_of(i * CHUNK * 16 + 16 * t, 16), 16), :] = b

        pair_new[i] = pair_chunk(pair_in[i], half_in, w_out, bias_t, g_pair, g_bias, ones, put_bias)
        write(i).start()
        for t in range(first // CHUNK):
            @pl.when(i == t * count // (first // CHUNK))
            def _():
                fetch(t).wait()
                hand_on(t).start()

        return carry

    lax.fori_loop(0, count, step, 0)
    for i in range(count):
        write(i).wait()
    for i in range(first // CHUNK):
        hand_on(i).wait()


def attend_kernel(
    q_ref, k_ref, v_ref, bias_early, bias_late, mask_ref, w_out, token_ref,
    out_ref,
    bias_ref,
    num_out, st_out, num_in, st_in, num_s, num_r, st_s, st_r,
):
    row, col = lax.axis_index("row"), lax.axis_index("col")
    barrier = pltpu.get_barrier_semaphore()
    for d in range(1, COLS):
        greet(barrier, row, (col + d) % COLS)

    split = bias_early.shape[0]
    bias_ref[:split] = bias_early[...]
    bias_ref[split:] = bias_late[...]
    head = lax.broadcasted_iota(jnp.int32, (16, 768), 0)
    lane = lax.broadcasted_iota(jnp.int32, (16, 768), 1)
    heads = jnp.where((lane >= head * HEAD) & (lane < head * HEAD + HEAD), 1.0, 0.0)
    eye = jnp.where(
        lax.broadcasted_iota(jnp.int32, (16, 128), 0) == lax.broadcasted_iota(jnp.int32, (16, 128), 1),
        1.0, 0.0,
    )
    masking = (mask_ref[...].astype(F32) - 1.0) * 1e9

    def chunk(c2):
        qs = q_ref[pl.ds(c2 * OWN, OWN), :].astype(F32)
        big = (qs[:, None, :] * heads[None]).reshape(256, 768).astype(BF16)
        s = dot_nt(big, k_ref[...]) * (HEAD ** -0.5)
        s = s + bias_ref[pl.ds(c2 * 256, 256), :] + masking
        top = jnp.max(s, axis=-1, keepdims=True)
        e = jnp.exp(s - top)
        total = jnp.sum(e, axis=-1, keepdims=True)
        o = dot(e.astype(BF16), v_ref[...])
        num = jnp.sum(o.reshape(OWN, 16, 768) * heads[None], axis=1)
        tops = jnp.sum(jnp.broadcast_to(top, (256, 128)).reshape(OWN, 16, 128) * eye[None], axis=1)
        totals = jnp.sum(jnp.broadcast_to(total, (256, 128)).reshape(OWN, 16, 128) * eye[None], axis=1)
        return num.astype(BF16), jnp.concatenate([tops, totals], axis=0)

    def send(d):
        c2 = (col + d) % COLS
        return (
            remote(num_out.at[c2], num_in.at[col], num_s.at[d], num_r.at[col], row, c2),
            remote(st_out.at[c2], st_in.at[col], st_s.at[d], st_r.at[col], row, c2),
        )

    def receive(d):
        c2 = (col + d) % COLS
        return (
            remote(num_out.at[c2], num_in.at[c2], num_s.at[d], num_r.at[c2], row, col),
            remote(st_out.at[c2], st_in.at[c2], st_s.at[d], st_r.at[c2], row, col),
        )

    for d in range(1, COLS):
        c2 = (col + d) % COLS
        num, st = chunk(c2)
        num_out[pl.ds(c2, 1)] = num[None]
        st_out[pl.ds(c2, 1)] = st[None]
        if d == 1:
            pl.semaphore_wait(barrier, COLS - 1)
        for copy in send(d):
            copy.start()
    num, st = chunk(col)
    num_in[pl.ds(col, 1)] = num[None]
    st_in[pl.ds(col, 1)] = st[None]
    for d in range(1, COLS):
        for copy in receive(d):
            copy.wait_recv()
    st = st_in[...]
    tops, totals = st[:, :OWN], st[:, OWN:]
    best = jnp.max(tops, axis=0, keepdims=True)
    w = jnp.exp(tops - best)
    den = jnp.sum(w * totals, axis=0)
    small = jnp.concatenate([w.reshape(COLS * OWN, 128), den], axis=0)
    wide = jnp.concatenate([heads, jnp.zeros((112, 768), F32)], axis=0)
    spread = jnp.dot(small, wide, preferred_element_type=F32, precision=lax.Precision.HIGHEST)
    num = jnp.zeros((OWN, 768), F32)
    for s in range(COLS):
        num = num + num_in[s].astype(F32) * spread[s * OWN:(s + 1) * OWN]
    mix = (num / spread[COLS * OWN:]).astype(BF16)
    out_ref[...] = (token_ref[...].astype(F32) + dot(mix, w_out[...])).astype(BF16)
    for d in range(1, COLS):
        for copy in send(d):
            copy.wait_send()


def body(
    atom_single, atom_to_token, token_mask, pair, w_atom_qkv, w_atom_out, w_aggregate,
    pair_gain, w_pair_in, w_pair_out, bias_gain, w_bias, token_gain, w_token_qkv, w_token_out,
):
    vmem = pl.BlockSpec(memory_space=pltpu.VMEM)
    anywhere = pl.BlockSpec(memory_space=pl.ANY)
    dma = pltpu.SemaphoreType.DMA
    nq, keys, chan = pair.shape
    early, late = EARLY, nq // CHUNK - EARLY
    g_pair, g_bias = pair_gain.reshape(1, chan), bias_gain.reshape(1, chan)
    prepared = [
        pltpu.VMEM((128, 512), BF16), pltpu.VMEM((128, 128), BF16),
    ]
    atom_out, token_in, q, k, v, done, bias_early = pl.pallas_call(
        tokens_kernel,
        in_specs=[anywhere] * 13,
        out_specs=[vmem] * 5 + [anywhere, vmem],
        out_shape=[
            jax.ShapeDtypeStruct((128, 128), BF16),
            jax.ShapeDtypeStruct((OWN, 768), BF16),
            jax.ShapeDtypeStruct((128, 768), BF16),
            jax.ShapeDtypeStruct((256, 768), BF16),
            jax.ShapeDtypeStruct((256, 768), BF16),
            jax.ShapeDtypeStruct((early * CHUNK, keys, chan), BF16),
            jax.ShapeDtypeStruct((early * CHUNK * 16, keys), F32),
        ],
        scratch_shapes=[
            pltpu.VMEM((128, 128), BF16), pltpu.VMEM((128, 128), jnp.int32),
            pltpu.VMEM((128, 384), BF16), pltpu.VMEM((128, 128), BF16),
            pltpu.VMEM((128, 768), BF16), pltpu.VMEM((6, 128), F32),
            pltpu.VMEM((768, 2304), BF16),
            pltpu.VMEM((128, 512), BF16), pltpu.VMEM((256, 128), BF16),
            pltpu.VMEM((16, 128), BF16), pltpu.VMEM((1, 128), F32), pltpu.VMEM((1, 128), F32),
            *prepared,
            pltpu.VMEM((early, CHUNK, keys, chan), BF16),
            pltpu.VMEM((early, CHUNK, keys, chan), BF16),
            pltpu.VMEM((224, 128), BF16),
            pltpu.VMEM((ROWS, 128, 128), BF16),
            pltpu.VMEM((COLS, OWN, 768), SUM_TYPE),
            pltpu.VMEM((COLS, OWN, 768), SUM_TYPE),
            pltpu.VMEM((OWN, 128), F32),
            pltpu.VMEM((OWN, 768), BF16),
            pltpu.VMEM((OWN, 768), BF16),
            pltpu.VMEM((OWN, 768), BF16),
            pltpu.VMEM((OWN, 768), BF16),
            pltpu.VMEM((COLS, OWN, 768), BF16),
            pltpu.VMEM((ROWS, OWN, 768), BF16),
            dma((12,)), dma((early,)), dma((early,)),
            dma((2,)), dma((2,)), dma((ROWS,)), dma((ROWS,)), dma((COLS,)), dma((COLS,)),
            dma((1,)), dma((1,)), dma((COLS,)), dma((COLS,)), dma((ROWS,)), dma((ROWS,)),
        ],
        compiler_params=pltpu.CompilerParams(
            collective_id=0, has_side_effects=True, vmem_limit_bytes=VMEM_LIMIT
        ),
        name="tokens",
    )(
        atom_single, atom_to_token.reshape(128, 128), w_atom_qkv, w_atom_out, w_aggregate,
        token_gain.reshape(6, 128), w_token_qkv,
        pair, w_pair_in, w_pair_out, w_bias.T, g_pair, g_bias,
    )
    pair_out, bias_late = pl.pallas_call(
        rest_kernel,
        in_specs=[anywhere, anywhere] + [vmem] * 5,
        out_specs=[anywhere, vmem],
        out_shape=[
            jax.ShapeDtypeStruct(pair.shape, BF16),
            jax.ShapeDtypeStruct((late * CHUNK * 16, keys), F32),
        ],
        scratch_shapes=[
            *prepared,
            pltpu.VMEM((late, CHUNK, keys, chan), BF16),
            pltpu.VMEM((late, CHUNK, keys, chan), BF16),
            pltpu.VMEM((early, CHUNK, keys, chan), BF16),
            dma((late,)), dma((late,)), dma((early,)), dma((early,)),
        ],
        compiler_params=pltpu.CompilerParams(vmem_limit_bytes=VMEM_LIMIT),
        name="pair",
    )(pair, done, w_pair_in, w_pair_out, w_bias.T, g_pair, g_bias)
    token_out = pl.pallas_call(
        attend_kernel,
        in_specs=[vmem] * 8,
        out_specs=vmem,
        out_shape=jax.ShapeDtypeStruct((OWN, 768), BF16),
        scratch_shapes=[
            pltpu.VMEM((nq * 16, keys), F32),
            pltpu.VMEM((COLS, OWN, 768), BF16),
            pltpu.VMEM((COLS, 2 * OWN, 128), F32),
            pltpu.VMEM((COLS, OWN, 768), BF16),
            pltpu.VMEM((COLS, 2 * OWN, 128), F32),
            dma((COLS,)), dma((COLS,)), dma((COLS,)), dma((COLS,)),
        ],
        compiler_params=pltpu.CompilerParams(
            collective_id=1, has_side_effects=True, vmem_limit_bytes=VMEM_LIMIT
        ),
        name="attend",
    )(q, k, v, bias_early, bias_late, token_mask.reshape(1, 256), w_token_out, token_in)
    return (atom_out, token_out, pair_out)


def solution(mesh):
    atoms = P(("row", "col"), None)
    pairs = P("row", "col", None)
    return jax.shard_map(
        body,
        mesh=mesh,
        in_specs=(atoms, P(), P("col"), pairs) + (P(),) * 11,
        out_specs=(atoms, atoms, pairs),
        check_vma=False,
    )
```

```python
import functools

import jax
import jax.numpy as jnp
from jax import lax
from jax.experimental import pallas as pl
from jax.experimental.pallas import tpu as pltpu
from jax.sharding import PartitionSpec as P

F32, BF16 = jnp.float32, jnp.bfloat16
MESH = pl.DeviceIdType.MESH
NT = (((1,), (1,)), ((), ()))
ROWS, COLS = 16, 8
WINDOW, KEYS, HALO = 32, 128, 48
ATOM_HEADS, TOKEN_HEADS, HEAD = 4, 16, 48
OWN = 16
VMEM_LIMIT = 56 << 20
SUM_TYPE = BF16
CHUNK = 16
BEFORE = 6
GROUPS = (6,)
STAGES = (0, 1, 3, 4)


def dot(a, b):
    return jnp.dot(a, b, preferred_element_type=F32)


def dot_nt(a, b):
    return lax.dot_general(a, b, NT, preferred_element_type=F32)


def remote(src, dst, send, recv, row, col):
    return pltpu.make_async_remote_copy(
        src_ref=src, dst_ref=dst, send_sem=send, recv_sem=recv,
        device_id=(row, col), device_id_type=MESH,
    )


def greet(sem, row, col):
    pl.semaphore_signal(sem, inc=1, device_id=(row, col), device_id_type=MESH)


def atom_attention(x, me, atoms_total, w_qkv, w_out):
    n = 128
    qkv = dot(x, w_qkv).astype(BF16)
    q = qkv[HALO:HALO + n, :128]
    k, v = qkv[:, 128:256], qkv[:, 256:]
    pad = jnp.zeros((256 - k.shape[0], 128), BF16)
    k = jnp.concatenate([k, pad], axis=0)
    v = jnp.concatenate([v, pad], axis=0)
    lane = lax.broadcasted_iota(jnp.int32, (n, 128), 1)
    parts = []
    for h in range(ATOM_HEADS):
        keep = (lane >= 32 * h) & (lane < 32 * h + 32)
        parts.append(jnp.where(keep, q.astype(F32), 0.0).astype(BF16))
    s = dot_nt(jnp.concatenate(parts, axis=0), k) * (32.0 ** -0.5)
    atom = lax.broadcasted_iota(jnp.int32, (n, 256), 0)
    key = lax.broadcasted_iota(jnp.int32, (n, 256), 1)
    first = (atom // WINDOW) * WINDOW
    place = key - HALO + me * n
    shift = jnp.where((place >= 0) & (place < atoms_total), 0.0, -1e9)
    inside = (key >= first) & (key < first + KEYS)
    out = jnp.zeros((n, 128), F32)
    for h in range(ATOM_HEADS):
        sh = jnp.where(inside, s[h * n:(h + 1) * n] + shift, -1e30)
        e = jnp.exp(sh - jnp.max(sh, axis=-1, keepdims=True))
        total = jnp.sum(e, axis=-1, keepdims=True)
        o = dot(e.astype(BF16), v) / total
        keep = (lane >= 32 * h) & (lane < 32 * h + 32)
        out = jnp.where(keep, o, out)
    own = x[HALO:HALO + n].astype(F32)
    return (own + dot(out.astype(BF16), w_out)).astype(BF16)


def norm_rows(x_bf, gain, ones):
    x = x_bf.astype(F32)
    xc = x - dot(x_bf, ones)
    var = jnp.mean(xc * xc, axis=-1, keepdims=True)
    return x, (xc * lax.rsqrt(var + 1e-5) * gain).astype(BF16)


def pair_weights(w_in, half_in, ones):
    half_in[:, :256] = w_in[:, :256] * jnp.asarray(0.5, BF16)
    half_in[:, 256:] = w_in[:, 256:]
    ones[...] = jnp.full(ones.shape, 1.0 / 128.0, BF16)


def pair_chunk(x, w_in, w_out, bias_t, g_pair, g_bias, ones, put_bias):
    n, keys, chan = x.shape
    x, normed = norm_rows(x.reshape(n * keys, chan), g_pair[...], ones[...])
    both = dot(normed, w_in[...])
    half, up = both[:, :256], both[:, 256:]
    hidden = ((half + half * jnp.tanh(half)) * up).astype(BF16)
    new = (x + dot(hidden, w_out[...])).astype(BF16)
    _, normed = norm_rows(new, g_bias[...], ones[...])
    for t in range(n):
        put_bias(t, dot_nt(bias_t[...], normed[t * keys:(t + 1) * keys]))
    return new.reshape(n, keys, chan)


def token_norm(t, gain):
    gain = jnp.concatenate([gain[i:i + 1] for i in range(6)], axis=1)
    t = t.astype(F32)
    tc = t - jnp.mean(t, axis=-1, keepdims=True)
    var = jnp.mean(tc * tc, axis=-1, keepdims=True)
    return (tc * lax.rsqrt(var + 1e-5) * gain).astype(BF16)


def step_kernel(
    atom_hbm, ids_hbm, w_aqkv_hbm, w_aout_hbm, w_agg_hbm, gain_hbm, w_qkv_hbm, mask_hbm,
    pair_hbm, w_in_hbm, w_out_hbm, bias_t_hbm, g_pair_hbm, g_bias_hbm,
    atom_out_hbm, token_hbm, num_hbm, pair_out_hbm,
    atom, ids, w_aqkv, w_aout, w_agg, gain, w_qkv, mask, w_in, w_out, bias_t, g_pair, g_bias,
    half_in, ones, pair_in, pair_new, bias,
    x_buf, gathered, sums, parts, counts, key_token, hot, tq, tk,
    query, key, value, num_out, num_in, atom_out,
    load, store, pair_r, pair_w,
    halo_s, halo_r, gat_s, gat_r, sum_s, sum_r, tq_s, tq_r, tk_s, tk_r,
    num_s, num_r,
):
    row, col = lax.axis_index("row"), lax.axis_index("col")
    me = row * COLS + col
    left, right = (me + 127) % 128, (me + 1) % 128
    twin = row + 1 - 2 * (row % 2)
    q_row, q_col = 2 * col + row // COLS, row // 2
    stays = (q_row == row).astype(jnp.int32)

    pairs = [
        (w_in_hbm, w_in), (w_out_hbm, w_out), (bias_t_hbm, bias_t), (g_pair_hbm, g_pair),
        (g_bias_hbm, g_bias), (atom_hbm, atom), (ids_hbm, ids), (w_aqkv_hbm, w_aqkv),
        (w_aout_hbm, w_aout), (w_agg_hbm, w_agg), (gain_hbm, gain), (w_qkv_hbm, w_qkv),
        (mask_hbm, mask),
    ]
    loads = [pltpu.make_async_copy(a, b, load.at[i]) for i, (a, b) in enumerate(pairs)]
    chunks = pair_in.shape[0]

    def owner(i):
        return (col + 1 + i) % COLS

    def rows_of(i):
        return pl.ds(pl.multiple_of(owner(i) * CHUNK, CHUNK), CHUNK)

    def read(i):
        return pltpu.make_async_copy(pair_hbm.at[rows_of(i)], pair_in.at[i], pair_r.at[i])

    def write(i):
        return pltpu.make_async_copy(pair_new.at[i], pair_out_hbm.at[pl.ds(i * CHUNK, CHUNK)], pair_w.at[i])

    loads[5].start()
    for copy in loads[:5]:
        copy.start()
    read(0).start()
    for copy in loads[6:]:
        copy.start()
    for i in range(1, chunks):
        read(i).start()

    barrier = pltpu.get_barrier_semaphore()
    greet(barrier, left // COLS, left % COLS)
    greet(barrier, right // COLS, right % COLS)
    greet(barrier, twin, col)
    for d in range(2, ROWS, 2):
        greet(barrier, (row + d) % ROWS, col)
    for d in range(1, COLS):
        greet(barrier, row, (col + d) % COLS)

    for i in range(COLS):
        @pl.when((stays == 0) | (row % COLS != i))
        def _():
            greet(barrier, COLS * (row % 2) + i, q_col)

    to_right = remote(atom.at[pl.ds(80, 48)], x_buf.at[pl.ds(0, 48)],
                      halo_s.at[0], halo_r.at[0], right // COLS, right % COLS)
    to_left = remote(atom.at[pl.ds(0, 48)], x_buf.at[pl.ds(176, 48)],
                     halo_s.at[1], halo_r.at[1], left // COLS, left % COLS)

    core, chip = row % 2, row // 2

    def spread(buf, send, recv, d):
        block = buf.at[core, chip]
        return remote(block, block, send.at[d], recv.at[chip], (row + 2 * d) % ROWS, col)

    def arrival(buf, send, recv, j):
        block = buf.at[core, j]
        return remote(block, block, send.at[0], recv.at[j], row, col)

    def hand_over(buf, send, recv, half, c):
        blocks = buf.at[c, pl.ds(4 * half, 4)]
        return remote(blocks, blocks, send.at[8 + half], recv.at[8 + half], twin, col)

    def start_spread(buf, send, recv):
        for d in range(1, 8):
            spread(buf, send, recv, d).start()

    def pass_on(buf, send, recv, half):
        for j in range(4 * half, 4 * half + 4):
            @pl.when(chip != j)
            def _():
                arrival(buf, send, recv, j).wait_recv()

        hand_over(buf, send, recv, half, core).start()

    def handed(buf, send, recv, half):
        hand_over(buf, send, recv, half, 1 - core).wait_recv()

    def drain_spread(buf, send, recv):
        for d in range(1, 8):
            spread(buf, send, recv, d).wait_send()
        for half in range(2):
            hand_over(buf, send, recv, half, core).wait_send()

    atoms_move = (gathered, gat_s, gat_r)
    keys_move = (tk, tk_s, tk_r)

    def send_sum(d):
        c2 = (col + d) % COLS
        return remote(sums.at[c2], parts.at[col], sum_s.at[d], sum_r.at[col], row, c2)

    def recv_sum(d):
        c2 = (col + d) % COLS
        return remote(sums.at[c2], parts.at[c2], sum_s.at[d], sum_r.at[c2], row, col)

    def send_q(d):
        return remote(key_token, tq.at[row % COLS], tq_s.at[d], tq_r.at[row % COLS], q_row, (col + d) % COLS)

    def recv_q(i):
        return remote(key_token, tq.at[i], tq_s.at[i], tq_r.at[i], row, col)

    def start_gather():
        for copy in loads[6:]:
            copy.wait()
        to_right.wait()
        to_left.wait()
        atom_out[...] = atom_attention(x_buf[...], me, 128 * 128, w_aqkv[...], w_aout[...])
        gathered[pl.ds(core, 1), pl.ds(chip, 1)] = atom_out[...][None, None]
        start_spread(*atoms_move)
        own_tokens = col * 256 + row * OWN + lax.broadcasted_iota(jnp.int32, (OWN, 128), 0)
        acc = jnp.zeros((OWN, 128), F32)
        for t in range(128):
            acc = acc + (own_tokens == ids[t:t + 1, :]).astype(F32)
        counts[...] = jnp.broadcast_to(jnp.sum(acc, axis=-1, keepdims=True), (OWN, 128))

        place = lax.broadcasted_iota(jnp.int32, (128, 128), 0)
        token = (place // OWN) * 256 + row * OWN + place % OWN
        for c in range(2):
            for j in range(8):
                here = ids[pl.ds(COLS * (2 * j + c) + col, 1), :]
                hot[c, :, 128 * j:128 * j + 128] = (token == here).astype(F32).astype(BF16)

    def part_sums(c, half):
        x = gathered[c, 4 * half:4 * half + 4].reshape(512, 128)
        proj = jnp.maximum(dot(x, w_agg[...]), 0.0).astype(BF16)
        return dot(hot[c, :, 512 * half:512 * half + 512], proj)

    def start_sums():
        pass_on(*atoms_move, 0)
        pass_on(*atoms_move, 1)
        total = part_sums(core, 0) + part_sums(core, 1)
        handed(*atoms_move, 0)
        total = total + part_sums(1 - core, 0)
        handed(*atoms_move, 1)
        total = total + part_sums(1 - core, 1)
        sums[...] = total.astype(sums.dtype).reshape(COLS, OWN, 768)
        for d in range(1, COLS):
            send_sum(d).start()
        parts[pl.ds(col, 1)] = sums[pl.ds(col, 1)]

    def start_keys():
        for d in range(1, COLS):
            recv_sum(d).wait_recv()
        acc = parts[0].astype(F32)
        for s in range(1, COLS):
            acc = acc + parts[s].astype(F32)
        token_in = (acc / counts[:, :1]).astype(BF16)
        key_token[...] = token_in
        tk[pl.ds(core, 1), pl.ds(chip, 1)] = token_norm(token_in, gain[...])[None, None]
        start_spread(*keys_move)
        for d in range(1, COLS):
            send_q(d).start()

        @pl.when(stays == 0)
        def _():
            send_q(0).start()

        @pl.when(stays == 1)
        def _():
            tq[pl.ds(row % COLS, 1)] = token_in[None]

    def pass_keys():
        pass_on(*keys_move, 0)
        pass_on(*keys_move, 1)

    stages = (start_gather, start_sums, start_keys, pass_keys)

    def pair_step(i):
        read(i).wait()

        def put_bias(t, b):
            bias[pl.ds(pl.multiple_of(i * CHUNK * 16 + 16 * t, 16), 16), :] = b

        pair_new[i] = pair_chunk(pair_in[i], half_in, w_out, bias_t, g_pair, g_bias, ones, put_bias)
        write(i).start()

    def step(i, carry):
        pair_step(i)
        for at, stage in zip(STAGES, stages):
            pl.when(i == at)(stage)
        return carry

    loads[5].wait()
    x_buf[HALO:HALO + 128] = atom[...]
    pl.semaphore_wait(barrier, 2 + 1 + 7 + 7 + 8 - stays)
    to_right.start()
    to_left.start()
    for copy in loads[:5]:
        copy.wait()
    pair_weights(w_in, half_in, ones)
    lax.fori_loop(0, BEFORE, step, 0)

    for i in range(COLS):
        @pl.when((stays == 0) | (row % COLS != i))
        def _():
            recv_q(i).wait_recv()

    for i in range(COLS):
        query[i * OWN:(i + 1) * OWN, :] = token_norm(tq[pl.ds(owner(i), 1)].reshape(OWN, 768), gain[...])
    query[...] = dot(query[...], w_qkv[:, :768]).astype(BF16)
    handed(*keys_move, 0)
    handed(*keys_move, 1)
    tkv = jnp.concatenate([tk[j % 2, j // 2] for j in range(ROWS)], axis=0)
    key[...] = dot(tkv, w_qkv[:, 768:1536]).astype(BF16)
    value[...] = dot(tkv, w_qkv[:, 1536:]).astype(BF16)

    results = [
        (atom_out, atom_out_hbm), (tq.at[col], token_hbm), (num_in, num_hbm),
    ]
    stores = [pltpu.make_async_copy(a, b, store.at[i]) for i, (a, b) in enumerate(results)]
    for copy in stores[:2]:
        copy.start()

    def send(i):
        return remote(num_out.at[i], num_in.at[col], num_s.at[i], num_r.at[col], row, owner(i))

    def receive(i):
        c2 = owner(i)
        return remote(num_out.at[i], num_in.at[c2], num_s.at[i], num_r.at[c2], row, col)

    def attend_slots(first, count):
        return attend(query[first * OWN:(first + count) * OWN, :],
                      bias[first * 256:(first + count) * 256, :], key, value, mask)

    def send_slots(first, count):
        num_out[first:first + count] = attend_slots(first, count)
        for i in range(first, first + count):
            send(i).start()

    first = 0
    for count in GROUPS:
        send_slots(first, count)
        first += count
    for i in range(first, chunks - 1):
        pair_step(i)
        send_slots(i, 1)
    if BEFORE < chunks:
        pair_step(chunks - 1)
    num_in[pl.ds(col, 1)] = attend_slots(chunks - 1, 1)

    drain_spread(*atoms_move)
    drain_spread(*keys_move)
    for d in range(1, COLS):
        send_sum(d).wait_send()
        send_q(d).wait_send()

    @pl.when(stays == 0)
    def _():
        send_q(0).wait_send()

    for i in range(chunks):
        write(i).wait()
    for i in range(COLS - 1):
        send(i).wait_send()
    for i in range(COLS - 1):
        receive(i).wait_recv()
    for copy in stores[2:]:
        copy.start()
    for copy in stores:
        copy.wait()


def head_lanes():
    head = lax.broadcasted_iota(jnp.int32, (16, 768), 0)
    lane = lax.broadcasted_iota(jnp.int32, (16, 768), 1)
    return jnp.where((lane >= head * HEAD) & (lane < head * HEAD + HEAD), 1.0, 0.0)


def pack_heads(column, n):
    lane = lax.broadcasted_iota(jnp.int32, (16, 128), 1)
    head = lax.broadcasted_iota(jnp.int32, (16, 128), 0)
    mine = jnp.where(lane % 16 == head, 1.0, 0.0)
    wide = jnp.sum(jnp.broadcast_to(column, (n * 16, 128)).reshape(n, 16, 128) * mine[None], axis=1)
    return jnp.sum(wide.reshape(n // 8, 8, 128) * token_lanes()[None], axis=1)


def token_lanes():
    lane = lax.broadcasted_iota(jnp.int32, (8, 128), 1)
    return jnp.where(lane // 16 == lax.broadcasted_iota(jnp.int32, (8, 128), 0), 1.0, 0.0)


def attend(query, bias, key, value, mask):
    n = query.shape[0]
    heads = head_lanes()
    masking = (mask[...].astype(F32) - 1.0) * 1e9
    big = (query.astype(F32)[:, None, :] * heads[None]).reshape(n * 16, 768).astype(BF16)
    s = dot_nt(big, key[...]) * (HEAD ** -0.5)
    s = s + bias + masking
    top = jnp.max(s, axis=-1, keepdims=True)
    e = jnp.exp(s - top)
    total = jnp.sum(e, axis=-1, keepdims=True)
    o = dot(e.astype(BF16), value[...])
    num = jnp.sum(o.reshape(n, 16, 768) * heads[None], axis=1).astype(BF16)
    tops, totals = pack_heads(top, n), pack_heads(total, n)
    parts = split_rows(tops, 3) + split_rows(totals, 2)
    rest = jnp.zeros((6, 128), F32)
    st = [
        jnp.concatenate([p[2 * i:2 * i + 2] for p in parts] + [rest], axis=0)
        for i in range(n // OWN)
    ]
    st = jnp.concatenate(st, axis=0).astype(BF16)
    return jnp.concatenate([num, st], axis=1).reshape(n // OWN, OWN, 896)


def split_rows(x, count):
    parts = []
    for _ in range(count):
        part = x.astype(BF16).astype(F32)
        parts.append(part)
        x = x - part
    return parts


def finish_kernel(
    done_hbm, atom_hbm, token_hbm, num_hbm, w_tout_hbm,
    pair_out_hbm, atom_out_hbm, token_out_hbm,
    atom, token, num_in, w_tout, held, token_out,
    load, done_r, done_w, store,
):
    col = lax.axis_index("col")
    count = held.shape[0]
    pairs = [(num_hbm, num_in), (w_tout_hbm, w_tout), (token_hbm, token), (atom_hbm, atom)]
    loads = [pltpu.make_async_copy(a, b, load.at[i]) for i, (a, b) in enumerate(pairs)]

    def rows_of(i):
        return pl.ds(pl.multiple_of((col + 1 + i) % COLS * CHUNK, CHUNK), CHUNK)

    def fetch(i):
        return pltpu.make_async_copy(done_hbm.at[pl.ds(i * CHUNK, CHUNK)], held.at[i], done_r.at[i])

    def hand_on(i):
        return pltpu.make_async_copy(held.at[i], pair_out_hbm.at[rows_of(i)], done_w.at[i])

    stores = [
        pltpu.make_async_copy(atom, atom_out_hbm, store.at[0]),
        pltpu.make_async_copy(token_out, token_out_hbm, store.at[1]),
    ]
    for i in range(count):
        fetch(i).start()
        if i == 1:
            for copy in loads:
                copy.start()
    for i in range(count):
        fetch(i).wait()
        hand_on(i).start()
    for copy in loads:
        copy.wait()
    stores[0].start()
    st = num_in[:, :, 768:].astype(F32)
    tops = st[:, 0:2] + st[:, 2:4] + st[:, 4:6]
    totals = st[:, 6:8] + st[:, 8:10]
    w = jnp.exp(tops - jnp.max(tops, axis=0, keepdims=True))
    den = jnp.sum(w * totals, axis=0)
    lanes = token_lanes()
    small = [
        jnp.broadcast_to(part[t:t + 1], (8, 128)) * lanes
        for part in [w[s] for s in range(COLS)] + [den] for t in range(2)
    ]
    wide = jnp.concatenate([head_lanes()] * 8, axis=0)
    spread = jnp.dot(jnp.concatenate(small, axis=0), wide, preferred_element_type=F32,
                     precision=lax.Precision.HIGHEST)
    acc = jnp.zeros((OWN, 768), F32)
    for s in range(COLS):
        acc = acc + num_in[s, :, :768].astype(F32) * spread[s * OWN:(s + 1) * OWN]
    mix = (acc / spread[COLS * OWN:]).astype(BF16)
    token_out[...] = (token[...].astype(F32) + dot(mix, w_tout[...])).astype(BF16)
    stores[1].start()
    for i in range(count):
        hand_on(i).wait()
    for copy in stores:
        copy.wait()


def body(
    atom_single, atom_to_token, token_mask, pair, w_atom_qkv, w_atom_out, w_aggregate,
    pair_gain, w_pair_in, w_pair_out, bias_gain, w_bias, token_gain, w_token_qkv, w_token_out,
):
    vmem = pl.BlockSpec(memory_space=pltpu.VMEM)
    anywhere = pl.BlockSpec(memory_space=pl.ANY)
    dma = pltpu.SemaphoreType.DMA
    nq, keys, chan = pair.shape
    chunks = nq // CHUNK
    block = pltpu.VMEM((OWN, 768), BF16)
    columns = pltpu.VMEM((COLS, OWN, 768), BF16)
    mixed = pltpu.VMEM((COLS, OWN, 896), BF16)
    taken = (CHUNK, keys, chan)
    pair_args = [
        pltpu.VMEM((128, 512), BF16), pltpu.VMEM((256, 128), BF16), pltpu.VMEM((16, 128), BF16),
        pltpu.VMEM((1, 128), F32), pltpu.VMEM((1, 128), F32),
    ]
    prepared = [pltpu.VMEM((128, 512), BF16), pltpu.VMEM((128, 128), BF16)]
    keyed = pltpu.VMEM((256, 768), BF16)
    pair_weights_in = (
        w_pair_in, w_pair_out, w_bias.T, pair_gain.reshape(1, chan), bias_gain.reshape(1, chan),
    )
    mask = token_mask.reshape(1, keys)
    atom_out, token_in, num, done = pl.pallas_call(
        step_kernel,
        in_specs=[anywhere] * 14,
        out_specs=[anywhere] * 4,
        out_shape=[
            jax.ShapeDtypeStruct((128, 128), BF16),
            jax.ShapeDtypeStruct((OWN, 768), BF16),
            jax.ShapeDtypeStruct((COLS, OWN, 896), BF16),
            jax.ShapeDtypeStruct(pair.shape, BF16),
        ],
        scratch_shapes=[
            pltpu.VMEM((128, 128), BF16), pltpu.VMEM((128, 128), jnp.int32),
            pltpu.VMEM((128, 384), BF16), pltpu.VMEM((128, 128), BF16),
            pltpu.VMEM((128, 768), BF16), pltpu.VMEM((6, 128), F32),
            pltpu.VMEM((768, 2304), BF16), pltpu.VMEM((1, 256), jnp.int32),
            *pair_args, *prepared,
            pltpu.VMEM((chunks, *taken), BF16),
            pltpu.VMEM((chunks, *taken), BF16),
            pltpu.VMEM((nq * 16, keys), F32),
            pltpu.VMEM((224, 128), BF16),
            pltpu.VMEM((2, 8, 128, 128), BF16),
            pltpu.VMEM((COLS, OWN, 768), SUM_TYPE),
            pltpu.VMEM((COLS, OWN, 768), SUM_TYPE),
            pltpu.VMEM((OWN, 128), F32),
            block, pltpu.VMEM((2, 128, 1024), BF16),
            columns,
            pltpu.VMEM((2, 8, OWN, 768), BF16),
            pltpu.VMEM((128, 768), BF16), keyed, keyed,
            mixed, mixed, pltpu.VMEM((128, 128), BF16),
            dma((13,)), dma((3,)), dma((chunks,)), dma((chunks,)),
            dma((2,)), dma((2,)), dma((16,)), dma((16,)), dma((COLS,)), dma((COLS,)),
            dma((COLS,)), dma((COLS,)), dma((16,)), dma((16,)),
            dma((COLS,)), dma((COLS,)),
        ],
        compiler_params=pltpu.CompilerParams(
            collective_id=0, has_side_effects=True, vmem_limit_bytes=VMEM_LIMIT
        ),
        name="step",
    )(
        atom_single, atom_to_token.reshape(128, 128), w_atom_qkv, w_atom_out, w_aggregate,
        token_gain.reshape(6, 128), w_token_qkv, mask, pair, *pair_weights_in,
    )
    pair_out, atom_out, token_out = pl.pallas_call(
        finish_kernel,
        in_specs=[anywhere] * 5,
        out_specs=[anywhere] * 3,
        out_shape=[
            jax.ShapeDtypeStruct(pair.shape, BF16),
            jax.ShapeDtypeStruct((128, 128), BF16),
            jax.ShapeDtypeStruct((OWN, 768), BF16),
        ],
        scratch_shapes=[
            pltpu.VMEM((128, 128), BF16), block, mixed, pltpu.VMEM((768, 768), BF16),
            pltpu.VMEM((chunks, *taken), BF16), block,
            dma((4,)), dma((chunks,)), dma((chunks,)), dma((2,)),
        ],
        compiler_params=pltpu.CompilerParams(vmem_limit_bytes=VMEM_LIMIT),
        name="finish",
    )(done, atom_out, token_in, num, w_token_out)
    return (atom_out, token_out, pair_out)


def solution(mesh):
    atoms = P(("row", "col"), None)
    pairs = P("row", "col", None)
    return jax.shard_map(
        body,
        mesh=mesh,
        in_specs=(atoms, P(), P("col"), pairs) + (P(),) * 11,
        out_specs=(atoms, atoms, pairs),
        check_vma=False,
    )
```

```python
import functools

import jax
import jax.numpy as jnp
from jax import lax
from jax.experimental import pallas as pl
from jax.experimental.pallas import tpu as pltpu
from jax.sharding import PartitionSpec as P

F32, BF16 = jnp.float32, jnp.bfloat16
MESH = pl.DeviceIdType.MESH
NT = (((1,), (1,)), ((), ()))
ROWS, COLS = 16, 8
WINDOW, KEYS, HALO = 32, 128, 48
ATOM_HEADS, TOKEN_HEADS, HEAD = 4, 16, 48
OWN = 16
VMEM_LIMIT = 48 << 20
SUM_TYPE = BF16
CHUNK = 16
BEFORE = 7
GROUPS = (4, 3)
STAGES = (0, 1, 3, 5)


def dot(a, b):
    return jnp.dot(a, b, preferred_element_type=F32)


def dot_nt(a, b):
    return lax.dot_general(a, b, NT, preferred_element_type=F32)


def remote(src, dst, send, recv, row, col):
    return pltpu.make_async_remote_copy(
        src_ref=src, dst_ref=dst, send_sem=send, recv_sem=recv,
        device_id=(row, col), device_id_type=MESH,
    )


def greet(sem, row, col):
    pl.semaphore_signal(sem, inc=1, device_id=(row, col), device_id_type=MESH)


def atom_attention(x, me, atoms_total, w_qkv, w_out):
    n = 128
    qkv = dot(x, w_qkv).astype(BF16)
    q = qkv[HALO:HALO + n, :128]
    k, v = qkv[:, 128:256], qkv[:, 256:]
    pad = jnp.zeros((256 - k.shape[0], 128), BF16)
    k = jnp.concatenate([k, pad], axis=0)
    v = jnp.concatenate([v, pad], axis=0)
    lane = lax.broadcasted_iota(jnp.int32, (n, 128), 1)
    parts = []
    for h in range(ATOM_HEADS):
        keep = (lane >= 32 * h) & (lane < 32 * h + 32)
        parts.append(jnp.where(keep, q.astype(F32), 0.0).astype(BF16))
    s = dot_nt(jnp.concatenate(parts, axis=0), k) * (32.0 ** -0.5)
    atom = lax.broadcasted_iota(jnp.int32, (n, 256), 0)
    key = lax.broadcasted_iota(jnp.int32, (n, 256), 1)
    first = (atom // WINDOW) * WINDOW
    place = key - HALO + me * n
    shift = jnp.where((place >= 0) & (place < atoms_total), 0.0, -1e9)
    inside = (key >= first) & (key < first + KEYS)
    out = jnp.zeros((n, 128), F32)
    for h in range(ATOM_HEADS):
        sh = jnp.where(inside, s[h * n:(h + 1) * n] + shift, -1e30)
        e = jnp.exp(sh - jnp.max(sh, axis=-1, keepdims=True))
        total = jnp.sum(e, axis=-1, keepdims=True)
        o = dot(e.astype(BF16), v) / total
        keep = (lane >= 32 * h) & (lane < 32 * h + 32)
        out = jnp.where(keep, o, out)
    own = x[HALO:HALO + n].astype(F32)
    return (own + dot(out.astype(BF16), w_out)).astype(BF16)


def norm_rows(x_bf, gain, ones):
    x = x_bf.astype(F32)
    xc = x - dot(x_bf, ones)
    var = jnp.mean(xc * xc, axis=-1, keepdims=True)
    return x, (xc * lax.rsqrt(var + 1e-5) * gain).astype(BF16)


def pair_weights(w_in, half_in, ones):
    half_in[:, :256] = w_in[:, :256] * jnp.asarray(0.5, BF16)
    half_in[:, 256:] = w_in[:, 256:]
    ones[...] = jnp.full(ones.shape, 1.0 / 128.0, BF16)


def pair_chunk(x, w_in, w_out, bias_t, g_pair, g_bias, ones, put_bias):
    n, keys, chan = x.shape
    x, normed = norm_rows(x.reshape(n * keys, chan), g_pair[...], ones[...])
    both = dot(normed, w_in[...])
    half, up = both[:, :256], both[:, 256:]
    hidden = ((half + half * jnp.tanh(half)) * up).astype(BF16)
    new = (x + dot(hidden, w_out[...])).astype(BF16)
    _, normed = norm_rows(new, g_bias[...], ones[...])
    for t in range(n):
        put_bias(t, dot_nt(bias_t[...], normed[t * keys:(t + 1) * keys]))
    return new.reshape(n, keys, chan)


def token_norm(t, gain):
    gain = jnp.concatenate([gain[i:i + 1] for i in range(6)], axis=1)
    t = t.astype(F32)
    tc = t - jnp.mean(t, axis=-1, keepdims=True)
    var = jnp.mean(tc * tc, axis=-1, keepdims=True)
    return (tc * lax.rsqrt(var + 1e-5) * gain).astype(BF16)


def step_kernel(
    atom_hbm, ids_hbm, w_aqkv_hbm, w_aout_hbm, w_agg_hbm, gain_hbm, w_qkv_hbm, mask_hbm,
    pair_hbm, w_in_hbm, w_out_hbm, bias_t_hbm, g_pair_hbm, g_bias_hbm,
    atom_out, token_out, num_final, pair_new,
    atom, ids, w_aqkv, w_aout, w_agg, gain, w_qkv, mask, w_in, w_out, bias_t, g_pair, g_bias,
    half_in, ones, pair_in, bias,
    x_buf, gathered, sums, parts, counts, key_token, hot, tq, tk,
    query, key, value, num_out, num_in,
    load, pair_r,
    halo_s, halo_r, gat_s, gat_r, sum_s, sum_r, tq_s, tq_r, tk_s, tk_r,
    num_s, num_r,
):
    row, col = lax.axis_index("row"), lax.axis_index("col")
    me = row * COLS + col
    left, right = (me + 127) % 128, (me + 1) % 128
    twin = row + 1 - 2 * (row % 2)
    q_row, q_col = 2 * col + row // COLS, row // 2
    stays = (q_row == row).astype(jnp.int32)

    pairs = [
        (w_in_hbm, w_in), (w_out_hbm, w_out), (bias_t_hbm, bias_t), (g_pair_hbm, g_pair),
        (g_bias_hbm, g_bias), (atom_hbm, atom), (ids_hbm, ids), (w_aqkv_hbm, w_aqkv),
        (w_aout_hbm, w_aout), (w_agg_hbm, w_agg), (gain_hbm, gain), (w_qkv_hbm, w_qkv),
        (mask_hbm, mask),
    ]
    loads = [pltpu.make_async_copy(a, b, load.at[i]) for i, (a, b) in enumerate(pairs)]
    chunks = pair_in.shape[0]

    def owner(i):
        return (col + 1 + i) % COLS

    def rows_of(i):
        return pl.ds(pl.multiple_of(owner(i) * CHUNK, CHUNK), CHUNK)

    def read(i):
        return pltpu.make_async_copy(pair_hbm.at[rows_of(i)], pair_in.at[i], pair_r.at[i])

    loads[5].start()
    for copy in loads[:5]:
        copy.start()
    read(0).start()
    for copy in loads[6:]:
        copy.start()
    for i in range(1, chunks):
        read(i).start()

    barrier = pltpu.get_barrier_semaphore()
    greet(barrier, left // COLS, left % COLS)
    greet(barrier, right // COLS, right % COLS)
    greet(barrier, twin, col)
    for d in range(2, ROWS, 2):
        greet(barrier, (row + d) % ROWS, col)
    for d in range(1, COLS):
        greet(barrier, row, (col + d) % COLS)

    for i in range(COLS):
        @pl.when((stays == 0) | (row % COLS != i))
        def _():
            greet(barrier, COLS * (row % 2) + i, q_col)

    to_right = remote(atom.at[pl.ds(80, 48)], x_buf.at[pl.ds(0, 48)],
                      halo_s.at[0], halo_r.at[0], right // COLS, right % COLS)
    to_left = remote(atom.at[pl.ds(0, 48)], x_buf.at[pl.ds(176, 48)],
                     halo_s.at[1], halo_r.at[1], left // COLS, left % COLS)

    core, chip = row % 2, row // 2

    def spread(buf, send, recv, d):
        block = buf.at[core, chip]
        return remote(block, block, send.at[d], recv.at[chip], (row + 2 * d) % ROWS, col)

    def arrival(buf, send, recv, j):
        block = buf.at[core, j]
        return remote(block, block, send.at[0], recv.at[j], row, col)

    def hand_over(buf, send, recv, half, c):
        blocks = buf.at[c, pl.ds(4 * half, 4)]
        return remote(blocks, blocks, send.at[8 + half], recv.at[8 + half], twin, col)

    def start_spread(buf, send, recv):
        for d in range(1, 8):
            spread(buf, send, recv, d).start()

    def pass_on(buf, send, recv, half):
        for j in range(4 * half, 4 * half + 4):
            @pl.when(chip != j)
            def _():
                arrival(buf, send, recv, j).wait_recv()

        hand_over(buf, send, recv, half, core).start()

    def handed(buf, send, recv, half):
        hand_over(buf, send, recv, half, 1 - core).wait_recv()

    def drain_spread(buf, send, recv):
        for d in range(1, 8):
            spread(buf, send, recv, d).wait_send()
        for half in range(2):
            hand_over(buf, send, recv, half, core).wait_send()

    atoms_move = (gathered, gat_s, gat_r)
    keys_move = (tk, tk_s, tk_r)

    def send_sum(d):
        c2 = (col + d) % COLS
        return remote(sums.at[c2], parts.at[col], sum_s.at[d], sum_r.at[col], row, c2)

    def recv_sum(d):
        c2 = (col + d) % COLS
        return remote(sums.at[c2], parts.at[c2], sum_s.at[d], sum_r.at[c2], row, col)

    def send_q(d):
        return remote(key_token, tq.at[row % COLS], tq_s.at[d], tq_r.at[row % COLS], q_row, (col + d) % COLS)

    def recv_q(i):
        return remote(key_token, tq.at[i], tq_s.at[i], tq_r.at[i], row, col)

    def start_gather():
        for copy in loads[6:]:
            copy.wait()
        to_right.wait()
        to_left.wait()
        atom_out[...] = atom_attention(x_buf[...], me, 128 * 128, w_aqkv[...], w_aout[...])
        gathered[pl.ds(core, 1), pl.ds(chip, 1)] = atom_out[...][None, None]
        start_spread(*atoms_move)
        own_tokens = col * 256 + row * OWN + lax.broadcasted_iota(jnp.int32, (OWN, 128), 0)
        acc = jnp.zeros((OWN, 128), F32)
        for t in range(128):
            acc = acc + (own_tokens == ids[t:t + 1, :]).astype(F32)
        counts[...] = jnp.broadcast_to(jnp.sum(acc, axis=-1, keepdims=True), (OWN, 128))

        place = lax.broadcasted_iota(jnp.int32, (128, 128), 0)
        token = (place // OWN) * 256 + row * OWN + place % OWN
        for c in range(2):
            for j in range(8):
                here = ids[pl.ds(COLS * (2 * j + c) + col, 1), :]
                hot[c, :, 128 * j:128 * j + 128] = (token == here).astype(F32).astype(BF16)

    def part_sums(c, half):
        x = gathered[c, 4 * half:4 * half + 4].reshape(512, 128)
        proj = jnp.maximum(dot(x, w_agg[...]), 0.0).astype(BF16)
        return dot(hot[c, :, 512 * half:512 * half + 512], proj)

    def start_sums():
        pass_on(*atoms_move, 0)
        pass_on(*atoms_move, 1)
        total = part_sums(core, 0) + part_sums(core, 1)
        handed(*atoms_move, 0)
        total = total + part_sums(1 - core, 0)
        handed(*atoms_move, 1)
        total = total + part_sums(1 - core, 1)
        sums[...] = total.astype(sums.dtype).reshape(COLS, OWN, 768)
        for d in range(1, COLS):
            send_sum(d).start()
        parts[pl.ds(col, 1)] = sums[pl.ds(col, 1)]

    def start_keys():
        for d in range(1, COLS):
            recv_sum(d).wait_recv()
        acc = parts[0].astype(F32)
        for s in range(1, COLS):
            acc = acc + parts[s].astype(F32)
        token_in = (acc / counts[:, :1]).astype(BF16)
        key_token[...] = token_in
        tk[pl.ds(core, 1), pl.ds(chip, 1)] = token_norm(token_in, gain[...])[None, None]
        start_spread(*keys_move)
        for d in range(1, COLS):
            send_q(d).start()

        @pl.when(stays == 0)
        def _():
            send_q(0).start()

        @pl.when(stays == 1)
        def _():
            tq[pl.ds(row % COLS, 1)] = token_in[None]

    def pass_keys():
        pass_on(*keys_move, 0)
        pass_on(*keys_move, 1)

    stages = (start_gather, start_sums, start_keys, pass_keys)

    def pair_step(i):
        read(i).wait()

        def put_bias(t, b):
            bias[pl.ds(pl.multiple_of(i * CHUNK * 16 + 16 * t, 16), 16), :] = b

        pair_new[i] = pair_chunk(pair_in[i], half_in, w_out, bias_t, g_pair, g_bias, ones, put_bias)

    def step(i, carry):
        pair_step(i)
        for at, stage in zip(STAGES, stages):
            pl.when(i == at)(stage)
        return carry

    loads[5].wait()
    x_buf[HALO:HALO + 128] = atom[...]
    pl.semaphore_wait(barrier, 2 + 1 + 7 + 7 + 8 - stays)
    to_right.start()
    to_left.start()
    for copy in loads[:5]:
        copy.wait()
    pair_weights(w_in, half_in, ones)
    lax.fori_loop(0, BEFORE, step, 0)

    for i in range(COLS):
        @pl.when((stays == 0) | (row % COLS != i))
        def _():
            recv_q(i).wait_recv()

    for i in range(COLS):
        query[i * OWN:(i + 1) * OWN, :] = token_norm(tq[pl.ds(owner(i), 1)].reshape(OWN, 768), gain[...])
    query[...] = dot(query[...], w_qkv[:, :768]).astype(BF16)
    handed(*keys_move, 0)
    handed(*keys_move, 1)
    tkv = jnp.concatenate([tk[j % 2, j // 2] for j in range(ROWS)], axis=0)
    key[...] = dot(tkv, w_qkv[:, 768:1536]).astype(BF16)
    value[...] = dot(tkv, w_qkv[:, 1536:]).astype(BF16)

    token_out[...] = tq[pl.ds(col, 1)].reshape(OWN, 768)

    def send(i):
        return remote(num_out.at[i], num_in.at[col], num_s.at[i], num_r.at[col], row, owner(i))

    def receive(i):
        c2 = owner(i)
        return remote(num_out.at[i], num_in.at[c2], num_s.at[i], num_r.at[c2], row, col)

    def attend_slots(first, count):
        return attend(query[first * OWN:(first + count) * OWN, :],
                      bias[first * 256:(first + count) * 256, :], key, value, mask)

    def send_slots(first, count):
        num_out[first:first + count] = attend_slots(first, count)
        for i in range(first, first + count):
            send(i).start()

    first = 0
    for count in GROUPS:
        send_slots(first, count)
        first += count
    for i in range(first, chunks - 1):
        pair_step(i)
        send_slots(i, 1)
    if BEFORE < chunks:
        pair_step(chunks - 1)
    num_in[pl.ds(col, 1)] = attend_slots(chunks - 1, 1)

    drain_spread(*atoms_move)
    drain_spread(*keys_move)
    for d in range(1, COLS):
        send_sum(d).wait_send()
        send_q(d).wait_send()

    @pl.when(stays == 0)
    def _():
        send_q(0).wait_send()

    for i in range(COLS - 1):
        send(i).wait_send()
    for i in range(COLS - 1):
        receive(i).wait_recv()
    num_final[...] = num_in[...]


def head_lanes():
    head = lax.broadcasted_iota(jnp.int32, (16, 768), 0)
    lane = lax.broadcasted_iota(jnp.int32, (16, 768), 1)
    return jnp.where((lane >= head * HEAD) & (lane < head * HEAD + HEAD), 1.0, 0.0)


def pack_heads(column, n):
    lane = lax.broadcasted_iota(jnp.int32, (16, 128), 1)
    head = lax.broadcasted_iota(jnp.int32, (16, 128), 0)
    mine = jnp.where(lane % 16 == head, 1.0, 0.0)
    wide = jnp.sum(jnp.broadcast_to(column, (n * 16, 128)).reshape(n, 16, 128) * mine[None], axis=1)
    return jnp.sum(wide.reshape(n // 8, 8, 128) * token_lanes()[None], axis=1)


def token_lanes():
    lane = lax.broadcasted_iota(jnp.int32, (8, 128), 1)
    return jnp.where(lane // 16 == lax.broadcasted_iota(jnp.int32, (8, 128), 0), 1.0, 0.0)


def attend(query, bias, key, value, mask):
    n = query.shape[0]
    heads = head_lanes()
    masking = (mask[...].astype(F32) - 1.0) * 1e9
    big = (query.astype(F32)[:, None, :] * heads[None]).reshape(n * 16, 768).astype(BF16)
    s = dot_nt(big, key[...]) * (HEAD ** -0.5)
    s = s + bias + masking
    top = jnp.max(s, axis=-1, keepdims=True)
    e = jnp.exp(s - top)
    total = jnp.sum(e, axis=-1, keepdims=True)
    o = dot(e.astype(BF16), value[...])
    num = jnp.sum(o.reshape(n, 16, 768) * heads[None], axis=1).astype(BF16)
    tops, totals = pack_heads(top, n), pack_heads(total, n)
    parts = split_rows(tops, 3) + split_rows(totals, 2)
    rest = jnp.zeros((6, 128), F32)
    st = [
        jnp.concatenate([p[2 * i:2 * i + 2] for p in parts] + [rest], axis=0)
        for i in range(n // OWN)
    ]
    st = jnp.concatenate(st, axis=0).astype(BF16)
    return jnp.concatenate([num, st], axis=1).reshape(n // OWN, OWN, 896)


def split_rows(x, count):
    parts = []
    for _ in range(count):
        part = x.astype(BF16).astype(F32)
        parts.append(part)
        x = x - part
    return parts


def finish_kernel(
    held, atom, token, num_in, w_tout_hbm,
    pair_out_hbm, atom_out_hbm, token_out_hbm,
    w_tout, token_out,
    load, done_w, store,
):
    col = lax.axis_index("col")
    count = held.shape[0]
    load_w = pltpu.make_async_copy(w_tout_hbm, w_tout, load.at[0])

    def rows_of(i):
        return pl.ds(pl.multiple_of((col + 1 + i) % COLS * CHUNK, CHUNK), CHUNK)

    def hand_on(i):
        return pltpu.make_async_copy(held.at[i], pair_out_hbm.at[rows_of(i)], done_w.at[i])

    stores = [
        pltpu.make_async_copy(atom, atom_out_hbm, store.at[0]),
        pltpu.make_async_copy(token_out, token_out_hbm, store.at[1]),
    ]
    load_w.start()
    for i in range(count):
        hand_on(i).start()
    stores[0].start()
    st = num_in[:, :, 768:].astype(F32)
    tops = st[:, 0:2] + st[:, 2:4] + st[:, 4:6]
    totals = st[:, 6:8] + st[:, 8:10]
    w = jnp.exp(tops - jnp.max(tops, axis=0, keepdims=True))
    den = jnp.sum(w * totals, axis=0)
    lanes = token_lanes()
    small = [
        jnp.broadcast_to(part[t:t + 1], (8, 128)) * lanes
        for part in [w[s] for s in range(COLS)] + [den] for t in range(2)
    ]
    wide = jnp.concatenate([head_lanes()] * 8, axis=0)
    spread = jnp.dot(jnp.concatenate(small, axis=0), wide, preferred_element_type=F32,
                     precision=lax.Precision.HIGHEST)
    acc = jnp.zeros((OWN, 768), F32)
    for s in range(COLS):
        acc = acc + num_in[s, :, :768].astype(F32) * spread[s * OWN:(s + 1) * OWN]
    mix = (acc / spread[COLS * OWN:]).astype(BF16)
    load_w.wait()
    token_out[...] = (token[...].astype(F32) + dot(mix, w_tout[...])).astype(BF16)
    stores[1].start()
    for i in range(count):
        hand_on(i).wait()
    for copy in stores:
        copy.wait()


def body(
    atom_single, atom_to_token, token_mask, pair, w_atom_qkv, w_atom_out, w_aggregate,
    pair_gain, w_pair_in, w_pair_out, bias_gain, w_bias, token_gain, w_token_qkv, w_token_out,
):
    vmem = pl.BlockSpec(memory_space=pltpu.VMEM)
    anywhere = pl.BlockSpec(memory_space=pl.ANY)
    dma = pltpu.SemaphoreType.DMA
    nq, keys, chan = pair.shape
    chunks = nq // CHUNK
    block = pltpu.VMEM((OWN, 768), BF16)
    columns = pltpu.VMEM((COLS, OWN, 768), BF16)
    mixed = pltpu.VMEM((COLS, OWN, 896), BF16)
    taken = (CHUNK, keys, chan)
    pair_args = [
        pltpu.VMEM((128, 512), BF16), pltpu.VMEM((256, 128), BF16), pltpu.VMEM((16, 128), BF16),
        pltpu.VMEM((1, 128), F32), pltpu.VMEM((1, 128), F32),
    ]
    prepared = [pltpu.VMEM((128, 512), BF16), pltpu.VMEM((128, 128), BF16)]
    keyed = pltpu.VMEM((256, 768), BF16)
    pair_weights_in = (
        w_pair_in, w_pair_out, w_bias.T, pair_gain.reshape(1, chan), bias_gain.reshape(1, chan),
    )
    mask = token_mask.reshape(1, keys)
    atom_out, token_in, num, done = pl.pallas_call(
        step_kernel,
        in_specs=[anywhere] * 14,
        out_specs=[vmem] * 4,
        out_shape=[
            pltpu.VMEM((128, 128), BF16), block, mixed, pltpu.VMEM((chunks, *taken), BF16),
        ],
        scratch_shapes=[
            pltpu.VMEM((128, 128), BF16), pltpu.VMEM((128, 128), jnp.int32),
            pltpu.VMEM((128, 384), BF16), pltpu.VMEM((128, 128), BF16),
            pltpu.VMEM((128, 768), BF16), pltpu.VMEM((6, 128), F32),
            pltpu.VMEM((768, 2304), BF16), pltpu.VMEM((1, 256), jnp.int32),
            *pair_args, *prepared,
            pltpu.VMEM((chunks, *taken), BF16),
            pltpu.VMEM((nq * 16, keys), F32),
            pltpu.VMEM((224, 128), BF16),
            pltpu.VMEM((2, 8, 128, 128), BF16),
            pltpu.VMEM((COLS, OWN, 768), SUM_TYPE),
            pltpu.VMEM((COLS, OWN, 768), SUM_TYPE),
            pltpu.VMEM((OWN, 128), F32),
            block, pltpu.VMEM((2, 128, 1024), BF16),
            columns,
            pltpu.VMEM((2, 8, OWN, 768), BF16),
            pltpu.VMEM((128, 768), BF16), keyed, keyed,
            mixed, mixed,
            dma((13,)), dma((chunks,)),
            dma((2,)), dma((2,)), dma((16,)), dma((16,)), dma((COLS,)), dma((COLS,)),
            dma((COLS,)), dma((COLS,)), dma((16,)), dma((16,)),
            dma((COLS,)), dma((COLS,)),
        ],
        compiler_params=pltpu.CompilerParams(
            collective_id=0, has_side_effects=True, vmem_limit_bytes=VMEM_LIMIT
        ),
        name="step",
    )(
        atom_single, atom_to_token.reshape(128, 128), w_atom_qkv, w_atom_out, w_aggregate,
        token_gain.reshape(6, 128), w_token_qkv, mask, pair, *pair_weights_in,
    )
    pair_out, atom_out, token_out = pl.pallas_call(
        finish_kernel,
        in_specs=[vmem] * 4 + [anywhere],
        out_specs=[anywhere] * 3,
        out_shape=[
            jax.ShapeDtypeStruct(pair.shape, BF16),
            jax.ShapeDtypeStruct((128, 128), BF16),
            jax.ShapeDtypeStruct((OWN, 768), BF16),
        ],
        scratch_shapes=[
            pltpu.VMEM((768, 768), BF16), block,
            dma((1,)), dma((chunks,)), dma((2,)),
        ],
        compiler_params=pltpu.CompilerParams(vmem_limit_bytes=16 << 20),
        name="finish",
    )(*[pltpu.with_memory_space_constraint(a, pltpu.VMEM) for a in (done, atom_out, token_in, num)], w_token_out)
    return (atom_out, token_out, pair_out)


def solution(mesh):
    atoms = P(("row", "col"), None)
    pairs = P("row", "col", None)
    return jax.shard_map(
        body,
        mesh=mesh,
        in_specs=(atoms, P(), P("col"), pairs) + (P(),) * 11,
        out_specs=(atoms, atoms, pairs),
        check_vma=False,
    )
```

```python
import functools

import jax
import jax.numpy as jnp
from jax import lax
from jax.experimental import pallas as pl
from jax.experimental.pallas import tpu as pltpu
from jax.sharding import PartitionSpec as P

F32, BF16 = jnp.float32, jnp.bfloat16
MESH = pl.DeviceIdType.MESH
NT = (((1,), (1,)), ((), ()))
ROWS, COLS = 16, 8
WINDOW, KEYS, HALO = 32, 128, 48
ATOM_HEADS, TOKEN_HEADS, HEAD = 4, 16, 48
OWN = 16
VMEM_LIMIT = 48 << 20
SUM_TYPE = BF16
CHUNK = 16
BEFORE = 7
GROUPS = (3, 2, 2)
STAGES = (0, 1, 3, 5)


def dot(a, b):
    return jnp.dot(a, b, preferred_element_type=F32)


def dot_nt(a, b):
    return lax.dot_general(a, b, NT, preferred_element_type=F32)


def remote(src, dst, send, recv, row, col):
    return pltpu.make_async_remote_copy(
        src_ref=src, dst_ref=dst, send_sem=send, recv_sem=recv,
        device_id=(row, col), device_id_type=MESH,
    )


def greet(sem, row, col):
    pl.semaphore_signal(sem, inc=1, device_id=(row, col), device_id_type=MESH)


def atom_attention(x, me, atoms_total, w_qkv, w_out):
    n = 128
    qkv = dot(x, w_qkv).astype(BF16)
    q = qkv[HALO:HALO + n, :128]
    k, v = qkv[:, 128:256], qkv[:, 256:]
    pad = jnp.zeros((256 - k.shape[0], 128), BF16)
    k = jnp.concatenate([k, pad], axis=0)
    v = jnp.concatenate([v, pad], axis=0)
    lane = lax.broadcasted_iota(jnp.int32, (n, 128), 1)
    parts = []
    for h in range(ATOM_HEADS):
        keep = (lane >= 32 * h) & (lane < 32 * h + 32)
        parts.append(jnp.where(keep, q.astype(F32), 0.0).astype(BF16))
    s = dot_nt(jnp.concatenate(parts, axis=0), k) * (32.0 ** -0.5)
    atom = lax.broadcasted_iota(jnp.int32, (n, 256), 0)
    key = lax.broadcasted_iota(jnp.int32, (n, 256), 1)
    first = (atom // WINDOW) * WINDOW
    place = key - HALO + me * n
    shift = jnp.where((place >= 0) & (place < atoms_total), 0.0, -1e9)
    inside = (key >= first) & (key < first + KEYS)
    out = jnp.zeros((n, 128), F32)
    for h in range(ATOM_HEADS):
        sh = jnp.where(inside, s[h * n:(h + 1) * n] + shift, -1e30)
        e = jnp.exp(sh - jnp.max(sh, axis=-1, keepdims=True))
        total = jnp.sum(e, axis=-1, keepdims=True)
        o = dot(e.astype(BF16), v) / total
        keep = (lane >= 32 * h) & (lane < 32 * h + 32)
        out = jnp.where(keep, o, out)
    own = x[HALO:HALO + n].astype(F32)
    return (own + dot(out.astype(BF16), w_out)).astype(BF16)


def norm_rows(x_bf, gain, ones):
    x = x_bf.astype(F32)
    xc = x - dot(x_bf, ones)
    var = jnp.mean(xc * xc, axis=-1, keepdims=True)
    return x, (xc * lax.rsqrt(var + 1e-5) * gain).astype(BF16)


def pair_weights(w_in, half_in, ones):
    half_in[:, :256] = w_in[:, :256] * jnp.asarray(0.5, BF16)
    half_in[:, 256:] = w_in[:, 256:]
    ones[...] = jnp.full(ones.shape, 1.0 / 128.0, BF16)


def pair_chunk(x, w_in, w_out, bias_t, g_pair, g_bias, ones, put_bias):
    n, keys, chan = x.shape
    x, normed = norm_rows(x.reshape(n * keys, chan), g_pair[...], ones[...])
    both = dot(normed, w_in[...])
    half, up = both[:, :256], both[:, 256:]
    hidden = ((half + half * jnp.tanh(half)) * up).astype(BF16)
    new = (x + dot(hidden, w_out[...])).astype(BF16)
    _, normed = norm_rows(new, g_bias[...], ones[...])
    for t in range(n):
        put_bias(t, dot_nt(bias_t[...], normed[t * keys:(t + 1) * keys]))
    return new.reshape(n, keys, chan)


def token_norm(t, gain):
    gain = jnp.concatenate([gain[i:i + 1] for i in range(6)], axis=1)
    t = t.astype(F32)
    tc = t - jnp.mean(t, axis=-1, keepdims=True)
    var = jnp.mean(tc * tc, axis=-1, keepdims=True)
    return (tc * lax.rsqrt(var + 1e-5) * gain).astype(BF16)


def step_kernel(
    atom_hbm, ids_hbm, w_aqkv_hbm, w_aout_hbm, w_agg_hbm, gain_hbm, w_qkv_hbm, mask_hbm,
    pair_hbm, w_in_hbm, w_out_hbm, bias_t_hbm, g_pair_hbm, g_bias_hbm,
    atom_out, token_out, num_final, pair_new,
    atom, ids, w_aqkv, w_aout, w_agg, gain, w_qkv, mask, w_in, w_out, bias_t, g_pair, g_bias,
    half_in, ones, pair_in, bias,
    x_buf, gathered, sums, parts, counts, key_token, hot, tq, tk,
    query, key, value, num_out, num_in,
    load, pair_r,
    halo_s, halo_r, gat_s, gat_r, sum_s, sum_r, tq_s, tq_r, tk_s, tk_r,
    num_s, num_r,
):
    row, col = lax.axis_index("row"), lax.axis_index("col")
    me = row * COLS + col
    left, right = (me + 127) % 128, (me + 1) % 128
    twin = row + 1 - 2 * (row % 2)
    q_row, q_col = 2 * col + row // COLS, row // 2
    stays = (q_row == row).astype(jnp.int32)

    pairs = [
        (w_in_hbm, w_in), (w_out_hbm, w_out), (bias_t_hbm, bias_t), (g_pair_hbm, g_pair),
        (g_bias_hbm, g_bias), (atom_hbm, atom), (ids_hbm, ids), (w_aqkv_hbm, w_aqkv),
        (w_aout_hbm, w_aout), (w_agg_hbm, w_agg), (gain_hbm, gain), (w_qkv_hbm, w_qkv),
        (mask_hbm, mask),
    ]
    loads = [pltpu.make_async_copy(a, b, load.at[i]) for i, (a, b) in enumerate(pairs)]
    chunks = pair_in.shape[0]

    def owner(i):
        return (col + 1 + i) % COLS

    def rows_of(i):
        return pl.ds(pl.multiple_of(owner(i) * CHUNK, CHUNK), CHUNK)

    def read(i):
        return pltpu.make_async_copy(pair_hbm.at[rows_of(i)], pair_in.at[i], pair_r.at[i])

    loads[5].start()
    for copy in loads[:5]:
        copy.start()
    read(0).start()
    for copy in loads[6:]:
        copy.start()
    for i in range(1, chunks):
        read(i).start()

    barrier = pltpu.get_barrier_semaphore()
    greet(barrier, left // COLS, left % COLS)
    greet(barrier, right // COLS, right % COLS)
    greet(barrier, twin, col)
    for d in range(2, ROWS, 2):
        greet(barrier, (row + d) % ROWS, col)
    for d in range(1, COLS):
        greet(barrier, row, (col + d) % COLS)

    for i in range(COLS):
        @pl.when((stays == 0) | (row % COLS != i))
        def _():
            greet(barrier, COLS * (row % 2) + i, q_col)

    to_right = remote(atom.at[pl.ds(80, 48)], x_buf.at[pl.ds(0, 48)],
                      halo_s.at[0], halo_r.at[0], right // COLS, right % COLS)
    to_left = remote(atom.at[pl.ds(0, 48)], x_buf.at[pl.ds(176, 48)],
                     halo_s.at[1], halo_r.at[1], left // COLS, left % COLS)

    core, chip = row % 2, row // 2

    def spread(buf, send, recv, d):
        block = buf.at[core, chip]
        return remote(block, block, send.at[d], recv.at[chip], (row + 2 * d) % ROWS, col)

    def arrival(buf, send, recv, j):
        block = buf.at[core, j]
        return remote(block, block, send.at[0], recv.at[j], row, col)

    def hand_over(buf, send, recv, half, c):
        blocks = buf.at[c, pl.ds(4 * half, 4)]
        return remote(blocks, blocks, send.at[8 + half], recv.at[8 + half], twin, col)

    def start_spread(buf, send, recv):
        for d in range(1, 8):
            spread(buf, send, recv, d).start()

    def pass_on(buf, send, recv, half):
        for j in range(4 * half, 4 * half + 4):
            @pl.when(chip != j)
            def _():
                arrival(buf, send, recv, j).wait_recv()

        hand_over(buf, send, recv, half, core).start()

    def handed(buf, send, recv, half):
        hand_over(buf, send, recv, half, 1 - core).wait_recv()

    def drain_spread(buf, send, recv):
        for d in range(1, 8):
            spread(buf, send, recv, d).wait_send()
        for half in range(2):
            hand_over(buf, send, recv, half, core).wait_send()

    atoms_move = (gathered, gat_s, gat_r)
    keys_move = (tk, tk_s, tk_r)

    def send_sum(d):
        c2 = (col + d) % COLS
        return remote(sums.at[c2], parts.at[col], sum_s.at[d], sum_r.at[col], row, c2)

    def recv_sum(d):
        c2 = (col + d) % COLS
        return remote(sums.at[c2], parts.at[c2], sum_s.at[d], sum_r.at[c2], row, col)

    def send_q(d):
        return remote(key_token, tq.at[row % COLS], tq_s.at[d], tq_r.at[row % COLS], q_row, (col + d) % COLS)

    def recv_q(i):
        return remote(key_token, tq.at[i], tq_s.at[i], tq_r.at[i], row, col)

    def start_gather():
        for copy in loads[6:]:
            copy.wait()
        to_right.wait()
        to_left.wait()
        atom_out[...] = atom_attention(x_buf[...], me, 128 * 128, w_aqkv[...], w_aout[...])
        gathered[pl.ds(core, 1), pl.ds(chip, 1)] = atom_out[...][None, None]
        start_spread(*atoms_move)
        own_tokens = col * 256 + row * OWN + lax.broadcasted_iota(jnp.int32, (OWN, 128), 0)
        acc = jnp.zeros((OWN, 128), F32)
        for t in range(128):
            acc = acc + (own_tokens == ids[t:t + 1, :]).astype(F32)
        counts[...] = jnp.broadcast_to(jnp.sum(acc, axis=-1, keepdims=True), (OWN, 128))

        place = lax.broadcasted_iota(jnp.int32, (128, 128), 0)
        token = (place // OWN) * 256 + row * OWN + place % OWN
        for c in range(2):
            for j in range(8):
                here = ids[pl.ds(COLS * (2 * j + c) + col, 1), :]
                hot[c, :, 128 * j:128 * j + 128] = (token == here).astype(F32).astype(BF16)

    def part_sums(c, half):
        x = gathered[c, 4 * half:4 * half + 4].reshape(512, 128)
        proj = jnp.maximum(dot(x, w_agg[...]), 0.0).astype(BF16)
        return dot(hot[c, :, 512 * half:512 * half + 512], proj)

    def start_sums():
        pass_on(*atoms_move, 0)
        pass_on(*atoms_move, 1)
        total = part_sums(core, 0) + part_sums(core, 1)
        handed(*atoms_move, 0)
        total = total + part_sums(1 - core, 0)
        handed(*atoms_move, 1)
        total = total + part_sums(1 - core, 1)
        sums[...] = total.astype(sums.dtype).reshape(COLS, OWN, 768)
        for d in range(1, COLS):
            send_sum(d).start()
        parts[pl.ds(col, 1)] = sums[pl.ds(col, 1)]

    def start_keys():
        for d in range(1, COLS):
            recv_sum(d).wait_recv()
        acc = parts[0].astype(F32)
        for s in range(1, COLS):
            acc = acc + parts[s].astype(F32)
        token_in = (acc / counts[:, :1]).astype(BF16)
        key_token[...] = token_in
        tk[pl.ds(core, 1), pl.ds(chip, 1)] = token_norm(token_in, gain[...])[None, None]
        start_spread(*keys_move)
        for d in range(1, COLS):
            send_q(d).start()

        @pl.when(stays == 0)
        def _():
            send_q(0).start()

        @pl.when(stays == 1)
        def _():
            tq[pl.ds(row % COLS, 1)] = token_in[None]

    def pass_keys():
        pass_on(*keys_move, 0)
        pass_on(*keys_move, 1)

    stages = (start_gather, start_sums, start_keys, pass_keys)

    def pair_step(i):
        read(i).wait()

        def put_bias(t, b):
            bias[pl.ds(pl.multiple_of(i * CHUNK * 16 + 16 * t, 16), 16), :] = b

        pair_new[i] = pair_chunk(pair_in[i], half_in, w_out, bias_t, g_pair, g_bias, ones, put_bias)

    def step(i, carry):
        pair_step(i)
        for at, stage in zip(STAGES, stages):
            pl.when(i == at)(stage)
        return carry

    loads[5].wait()
    x_buf[HALO:HALO + 128] = atom[...]
    pl.semaphore_wait(barrier, 2 + 1 + 7 + 7 + 8 - stays)
    to_right.start()
    to_left.start()
    for copy in loads[:5]:
        copy.wait()
    pair_weights(w_in, half_in, ones)
    lax.fori_loop(0, BEFORE, step, 0)

    for i in range(COLS):
        @pl.when((stays == 0) | (row % COLS != i))
        def _():
            recv_q(i).wait_recv()

    for i in range(COLS):
        query[i * OWN:(i + 1) * OWN, :] = token_norm(tq[pl.ds(owner(i), 1)].reshape(OWN, 768), gain[...])
    query[...] = dot(query[...], w_qkv[:, :768]).astype(BF16)
    handed(*keys_move, 0)
    handed(*keys_move, 1)
    tkv = jnp.concatenate([tk[j % 2, j // 2] for j in range(ROWS)], axis=0)
    key[...] = dot(tkv, w_qkv[:, 768:1536]).astype(BF16)
    value[...] = dot(tkv, w_qkv[:, 1536:]).astype(BF16)

    token_out[...] = tq[pl.ds(col, 1)].reshape(OWN, 768)

    def send(i):
        return remote(num_out.at[i], num_in.at[col], num_s.at[i], num_r.at[col], row, owner(i))

    def receive(i):
        c2 = owner(i)
        return remote(num_out.at[i], num_in.at[c2], num_s.at[i], num_r.at[c2], row, col)

    def attend_slots(first, count):
        return attend(query[first * OWN:(first + count) * OWN, :],
                      bias[first * 256:(first + count) * 256, :], key, value, mask)

    def send_slots(first, count):
        num_out[first:first + count] = attend_slots(first, count)
        for i in range(first, first + count):
            send(i).start()

    first = 0
    for count in GROUPS:
        send_slots(first, count)
        first += count
    for i in range(first, chunks - 1):
        pair_step(i)
        send_slots(i, 1)
    if BEFORE < chunks:
        pair_step(chunks - 1)
    num_in[pl.ds(col, 1)] = attend_slots(chunks - 1, 1)

    drain_spread(*atoms_move)
    drain_spread(*keys_move)
    for d in range(1, COLS):
        send_sum(d).wait_send()
        send_q(d).wait_send()

    @pl.when(stays == 0)
    def _():
        send_q(0).wait_send()

    for i in range(COLS - 1):
        send(i).wait_send()
    for i in range(COLS - 1):
        receive(i).wait_recv()
    num_final[...] = num_in[...]


def head_lanes():
    head = lax.broadcasted_iota(jnp.int32, (16, 768), 0)
    lane = lax.broadcasted_iota(jnp.int32, (16, 768), 1)
    return jnp.where((lane >= head * HEAD) & (lane < head * HEAD + HEAD), 1.0, 0.0)


def pack_heads(column, n):
    lane = lax.broadcasted_iota(jnp.int32, (16, 128), 1)
    head = lax.broadcasted_iota(jnp.int32, (16, 128), 0)
    mine = jnp.where(lane % 16 == head, 1.0, 0.0)
    wide = jnp.sum(jnp.broadcast_to(column, (n * 16, 128)).reshape(n, 16, 128) * mine[None], axis=1)
    return jnp.sum(wide.reshape(n // 8, 8, 128) * token_lanes()[None], axis=1)


def token_lanes():
    lane = lax.broadcasted_iota(jnp.int32, (8, 128), 1)
    return jnp.where(lane // 16 == lax.broadcasted_iota(jnp.int32, (8, 128), 0), 1.0, 0.0)


def attend(query, bias, key, value, mask):
    n = query.shape[0]
    heads = head_lanes()
    masking = (mask[...].astype(F32) - 1.0) * 1e9
    big = (query.astype(F32)[:, None, :] * heads[None]).reshape(n * 16, 768).astype(BF16)
    s = dot_nt(big, key[...]) * (HEAD ** -0.5)
    s = s + bias + masking
    top = jnp.max(s, axis=-1, keepdims=True)
    e = jnp.exp(s - top)
    total = jnp.sum(e, axis=-1, keepdims=True)
    o = dot(e.astype(BF16), value[...])
    num = jnp.sum(o.reshape(n, 16, 768) * heads[None], axis=1).astype(BF16)
    tops, totals = pack_heads(top, n), pack_heads(total, n)
    parts = split_rows(tops, 3) + split_rows(totals, 2)
    rest = jnp.zeros((6, 128), F32)
    st = [
        jnp.concatenate([p[2 * i:2 * i + 2] for p in parts] + [rest], axis=0)
        for i in range(n // OWN)
    ]
    st = jnp.concatenate(st, axis=0).astype(BF16)
    return jnp.concatenate([num, st], axis=1).reshape(n // OWN, OWN, 896)


def split_rows(x, count):
    parts = []
    for _ in range(count):
        part = x.astype(BF16).astype(F32)
        parts.append(part)
        x = x - part
    return parts


def finish_kernel(
    held, atom, token, num_in, w_tout_hbm,
    pair_out_hbm, atom_out_hbm, token_out_hbm,
    w_tout, token_out,
    load, done_w, store,
):
    col = lax.axis_index("col")
    count = held.shape[0]
    load_w = pltpu.make_async_copy(w_tout_hbm, w_tout, load.at[0])

    def rows_of(i):
        return pl.ds(pl.multiple_of((col + 1 + i) % COLS * CHUNK, CHUNK), CHUNK)

    def hand_on(i):
        return pltpu.make_async_copy(held.at[i], pair_out_hbm.at[rows_of(i)], done_w.at[i])

    stores = [
        pltpu.make_async_copy(atom, atom_out_hbm, store.at[0]),
        pltpu.make_async_copy(token_out, token_out_hbm, store.at[1]),
    ]
    load_w.start()
    for i in range(count):
        hand_on(i).start()
    stores[0].start()
    st = num_in[:, :, 768:].astype(F32)
    tops = st[:, 0:2] + st[:, 2:4] + st[:, 4:6]
    totals = st[:, 6:8] + st[:, 8:10]
    w = jnp.exp(tops - jnp.max(tops, axis=0, keepdims=True))
    den = jnp.sum(w * totals, axis=0)
    lanes = token_lanes()
    small = [
        jnp.broadcast_to(part[t:t + 1], (8, 128)) * lanes
        for part in [w[s] for s in range(COLS)] + [den] for t in range(2)
    ]
    wide = jnp.concatenate([head_lanes()] * 8, axis=0)
    spread = jnp.dot(jnp.concatenate(small, axis=0), wide, preferred_element_type=F32,
                     precision=lax.Precision.HIGHEST)
    acc = jnp.zeros((OWN, 768), F32)
    for s in range(COLS):
        acc = acc + num_in[s, :, :768].astype(F32) * spread[s * OWN:(s + 1) * OWN]
    mix = (acc / spread[COLS * OWN:]).astype(BF16)
    load_w.wait()
    token_out[...] = (token[...].astype(F32) + dot(mix, w_tout[...])).astype(BF16)
    stores[1].start()
    for i in range(count):
        hand_on(i).wait()
    for copy in stores:
        copy.wait()


def body(
    atom_single, atom_to_token, token_mask, pair, w_atom_qkv, w_atom_out, w_aggregate,
    pair_gain, w_pair_in, w_pair_out, bias_gain, w_bias, token_gain, w_token_qkv, w_token_out,
):
    vmem = pl.BlockSpec(memory_space=pltpu.VMEM)
    anywhere = pl.BlockSpec(memory_space=pl.ANY)
    dma = pltpu.SemaphoreType.DMA
    nq, keys, chan = pair.shape
    chunks = nq // CHUNK
    block = pltpu.VMEM((OWN, 768), BF16)
    columns = pltpu.VMEM((COLS, OWN, 768), BF16)
    mixed = pltpu.VMEM((COLS, OWN, 896), BF16)
    taken = (CHUNK, keys, chan)
    pair_args = [
        pltpu.VMEM((128, 512), BF16), pltpu.VMEM((256, 128), BF16), pltpu.VMEM((16, 128), BF16),
        pltpu.VMEM((1, 128), F32), pltpu.VMEM((1, 128), F32),
    ]
    prepared = [pltpu.VMEM((128, 512), BF16), pltpu.VMEM((128, 128), BF16)]
    keyed = pltpu.VMEM((256, 768), BF16)
    pair_weights_in = (
        w_pair_in, w_pair_out, w_bias.T, pair_gain.reshape(1, chan), bias_gain.reshape(1, chan),
    )
    mask = token_mask.reshape(1, keys)
    atom_out, token_in, num, done = pl.pallas_call(
        step_kernel,
        in_specs=[anywhere] * 14,
        out_specs=[vmem] * 4,
        out_shape=[
            pltpu.VMEM((128, 128), BF16), block, mixed, pltpu.VMEM((chunks, *taken), BF16),
        ],
        scratch_shapes=[
            pltpu.VMEM((128, 128), BF16), pltpu.VMEM((128, 128), jnp.int32),
            pltpu.VMEM((128, 384), BF16), pltpu.VMEM((128, 128), BF16),
            pltpu.VMEM((128, 768), BF16), pltpu.VMEM((6, 128), F32),
            pltpu.VMEM((768, 2304), BF16), pltpu.VMEM((1, 256), jnp.int32),
            *pair_args, *prepared,
            pltpu.VMEM((chunks, *taken), BF16),
            pltpu.VMEM((nq * 16, keys), F32),
            pltpu.VMEM((224, 128), BF16),
            pltpu.VMEM((2, 8, 128, 128), BF16),
            pltpu.VMEM((COLS, OWN, 768), SUM_TYPE),
            pltpu.VMEM((COLS, OWN, 768), SUM_TYPE),
            pltpu.VMEM((OWN, 128), F32),
            block, pltpu.VMEM((2, 128, 1024), BF16),
            columns,
            pltpu.VMEM((2, 8, OWN, 768), BF16),
            pltpu.VMEM((128, 768), BF16), keyed, keyed,
            mixed, mixed,
            dma((13,)), dma((chunks,)),
            dma((2,)), dma((2,)), dma((16,)), dma((16,)), dma((COLS,)), dma((COLS,)),
            dma((COLS,)), dma((COLS,)), dma((16,)), dma((16,)),
            dma((COLS,)), dma((COLS,)),
        ],
        compiler_params=pltpu.CompilerParams(
            collective_id=0, has_side_effects=True, vmem_limit_bytes=VMEM_LIMIT
        ),
        name="step",
    )(
        atom_single, atom_to_token.reshape(128, 128), w_atom_qkv, w_atom_out, w_aggregate,
        token_gain.reshape(6, 128), w_token_qkv, mask, pair, *pair_weights_in,
    )
    pair_out, atom_out, token_out = pl.pallas_call(
        finish_kernel,
        in_specs=[vmem] * 4 + [anywhere],
        out_specs=[anywhere] * 3,
        out_shape=[
            jax.ShapeDtypeStruct(pair.shape, BF16),
            jax.ShapeDtypeStruct((128, 128), BF16),
            jax.ShapeDtypeStruct((OWN, 768), BF16),
        ],
        scratch_shapes=[
            pltpu.VMEM((768, 768), BF16), block,
            dma((1,)), dma((chunks,)), dma((2,)),
        ],
        compiler_params=pltpu.CompilerParams(vmem_limit_bytes=16 << 20),
        name="finish",
    )(*[pltpu.with_memory_space_constraint(a, pltpu.VMEM) for a in (done, atom_out, token_in, num)], w_token_out)
    return (atom_out, token_out, pair_out)


def solution(mesh):
    atoms = P(("row", "col"), None)
    pairs = P("row", "col", None)
    return jax.shard_map(
        body,
        mesh=mesh,
        in_specs=(atoms, P(), P("col"), pairs) + (P(),) * 11,
        out_specs=(atoms, atoms, pairs),
        check_vma=False,
    )
```
